512 devices in a mesh: mem: 8 (over z_lo), hor: 64 (over z_hi, x, y, core).
Axes of the slice: x: 4, y: 4, z: 16 (z_hi: 2, z_lo: 8; z = z_hi * 8 + z_lo), core: 2. Of those that a mesh axis runs over, the one named last changes fastest.
Arguments:
- fine_increment: float32 [4, 4608, 768], P(None, 'hor', 'mem'), may hold values from -6 to 6
- row_taps: float32 [4, 2304], P(None, 'hor'), may hold values from 0 to 0.45, as said below
- col_weights: float32 [768, 384], replicated, may hold values from 0 to 0.45, as said below
- prior: bfloat16 [80, 4, 2304, 384], P('mem', None, 'hor'), may hold values from -6 to 6
- posterior: bfloat16 [80, 4, 2304, 384], P('mem', None, 'hor'), may hold values from -4 to 4
Outputs:
- recentred: bfloat16 [80, 4, 2304, 384], P('mem', None, 'hor')
The draws below stay inside these ranges and needn't reach their ends.
Inputs may be any that keep to these rules, and one draw needn't show every extreme that they name: row_taps[t, g] is zero where control-grid row 2 g - 1 + t lies outside rows 0 to 4607. Column c of col_weights is zero outside rows 2 c - 1 to 2 c + 2.
All inputs are finite; a program needn't handle non-finite values.
Results may differ from the reference program's by a relative error of at most 0.001.
Values sent between devices are 32-bit elements; how exact they have to be, the bound alone decides.
No kernel may reach another device: no remote copies, remote signals or barrier semaphores. Data moves between devices by JAX's collectives and lax.ppermute only.
A program may use at most 64 MiB of HBM per device.

```python
import jax
import jax.numpy as jnp
from jax import lax

NF = 768
NC = 384
FACES = 6
LEV = 4
MEMBERS = 80


def draw_row_taps(key, part):
    key = jax.random.fold_in(key, 11)
    values = jax.random.uniform(key, (4, FACES * NC), jnp.float32, 0.1, 0.45)
    coarse_rows = jnp.arange(FACES * NC)
    offsets = jnp.arange(4)[:, None]
    target = 2 * coarse_rows[None, :] - 1 + offsets
    inside = (target >= 0) & (target < FACES * NF)
    return jnp.where(inside, values, 0.0).astype(jnp.float32)


def draw_col_weights(key, part):
    key = jax.random.fold_in(key, 12)
    values = jax.random.uniform(key, (NF, NC), jnp.float32, 0.1, 0.45)
    rows_fine = jnp.arange(NF)[:, None]
    columns = jnp.arange(NC)[None, :]
    band = (rows_fine >= 2 * columns - 1) & (rows_fine <= 2 * columns + 2)
    return jnp.where(band, values, 0.0).astype(jnp.float32)


def levels(key, extent, shards, low, high):
    level, own = 1.0, jax.random.fold_in(key, 6)
    for position, parts in shards:
        draws = jnp.exp(jax.random.uniform(jax.random.fold_in(own, position), (parts,), jnp.float32, low / len(shards), high / len(shards)))
        level = level * jnp.repeat(draws, extent[position] // parts).reshape([-1 if axis == position else 1 for axis in range(len(extent))])
    return level


def centred(rng, dims, width, bound, pieces=(), kind=jnp.bfloat16):
    values = jax.random.normal(rng, dims, jnp.float32) * width
    if len(pieces) > 0:
        values = levels(rng, dims, pieces, -0.22, 0.18) * values
    return jnp.clip(values, min=-bound, max=bound).astype(kind)


def setup_inputs(seed: int = 0) -> dict:
    streams_of = jax.random.split(jax.random.key(seed), 6)
    fine_increment = centred(streams_of[0], (LEV, FACES * NF, NF), 1.0, 6.0, ((1, 64), (2, 8)), jnp.float32)
    row_taps = draw_row_taps(jax.random.fold_in(streams_of[5], 71), 0)
    col_weights = draw_col_weights(jax.random.fold_in(streams_of[5], 71), 0)
    prior = centred(streams_of[3], (MEMBERS, LEV, FACES * NC, NC), 1.0, 6.0, ((0, 8), (2, 64)))
    posterior = centred(streams_of[4], (MEMBERS, LEV, FACES * NC, NC), 0.6, 4.0, ((0, 8), (2, 64)))
    return {"fine_increment": fine_increment, "row_taps": row_taps, "col_weights": col_weights, "prior": prior, "posterior": posterior}


def restrict_rows(padded_rows, taps):
    count = taps.shape[1]
    total = taps[0][None, :, None] * padded_rows[:, 0:2 * count:2, :]
    for offset in range(1, 4):
        total = total + taps[offset][None, :, None] * padded_rows[:, offset:offset + 2 * count:2, :]
    return total

def reference(fine_increment, row_taps, col_weights, prior, posterior):
    colres = jnp.einsum('lrj,jc->lrc', fine_increment, col_weights, precision=lax.Precision.HIGHEST)
    padded = jnp.pad(colres, ((0, 0), (1, 1), (0, 0)))
    increment = restrict_rows(padded, row_taps)
    count = prior.shape[0]

    def per_level(items):
        before, after, shift = items
        before = before.astype(jnp.float32)
        after = after.astype(jnp.float32)
        prior_mean = lax.optimization_barrier(jnp.sum(before, axis=0)) / count
        post_mean = lax.optimization_barrier(jnp.sum(after, axis=0)) / count
        prior_var = lax.optimization_barrier(jnp.sum((before - prior_mean) ** 2, axis=0)) / (count - 1)
        post_var = lax.optimization_barrier(jnp.sum((after - post_mean) ** 2, axis=0)) / (count - 1)
        prior_spread = jnp.sqrt(prior_var + 1e-06)
        post_spread = jnp.sqrt(post_var + 1e-06)
        factor = 1.0 + 0.9 * (prior_spread - post_spread) / post_spread
        return (prior_mean + shift + factor * (after - post_mean)).astype(jnp.bfloat16)
    result = lax.map(per_level, (jnp.moveaxis(prior, 1, 0), jnp.moveaxis(posterior, 1, 0), increment))
    return jnp.moveaxis(result, 0, 1)
```

```python
import functools

import jax
import jax.numpy as jnp
from jax import lax
from jax.experimental import pallas as pl
from jax.experimental.pallas import tpu as pltpu
from jax.sharding import PartitionSpec as P

CHUNK = 56
ORDER = (0, 4, 2, 6, 1, 5, 3, 7)
F32 = jnp.float32
HIGHEST = lax.Precision.HIGHEST


def pack(ref, which, level, value):
    for e in range(2):
        base = (2 * level + e) * CHUNK
        for rt in range(2):
            for ct in range(3):
                at = base + (3 * rt + ct) * 8
                row = 16 * e + 8 * rt
                ref[which, at : at + 8, :] = value[row : row + 8, 128 * ct : 128 * ct + 128]
        for ct in range(3):
            at = base + 48 + 2 * ct
            ref[which, at : at + 2, :] = value[32 + 2 * e : 34 + 2 * e, 128 * ct : 128 * ct + 128]
        ref[which, base + 54 : base + 56, :] = jnp.zeros((2, 128), F32)


def stats_kernel(m_ref, x_ref, keep_ref, send_ref, all_ref):
    m = m_ref[0]
    members = x_ref.shape[0]
    for level in range(4):
        total = x_ref[0, level].astype(F32)
        for i in range(1, members):
            total = total + x_ref[i, level].astype(F32)
        mean = total / members
        square = jnp.zeros_like(total)
        for i in range(members):
            dev = x_ref[i, level].astype(F32) - mean
            square = square + dev * dev
        pack(all_ref, 0, level, total)
        pack(all_ref, 1, level, square)
    for p in range(8):
        at = pl.multiple_of((m ^ ORDER[p]) * CHUNK, 8)
        out, to = (keep_ref, p * CHUNK) if p < 4 else (send_ref, (p - 4) * CHUNK)
        for which in range(2):
            out[which, to : to + CHUNK, :] = all_ref[which, pl.ds(at, CHUNK), :]


def stats(m, x):
    shape = jax.ShapeDtypeStruct((2, 4 * CHUNK, 128), F32)
    return pl.pallas_call(
        stats_kernel,
        out_shape=(shape, shape),
        in_specs=[pl.BlockSpec(memory_space=pltpu.SMEM), pl.BlockSpec(memory_space=pltpu.VMEM)],
        out_specs=(pl.BlockSpec(memory_space=pltpu.VMEM),) * 2,
        scratch_shapes=[pltpu.VMEM((2, 8 * CHUNK, 128), F32)],
        compiler_params=pltpu.CompilerParams(vmem_limit_bytes=16 * 2**20),
        cost_estimate=pl.CostEstimate(flops=4_000_000, bytes_accessed=2_500_000, transcendentals=0),
        name="stats",
    )(m, x)


def fine_kernel(m_ref, fine_ref, up_ref, down_ref, taps_ref, weights_ref, keep_ref, send_ref, rows_ref, all_ref):
    m = m_ref[0]
    weights = weights_ref[pl.ds(pl.multiple_of(m * 96, 32), 96), :]
    local = pltpu.roll(weights, lax.rem(385 - 48 * m, 384), 1)[:, :128]
    for level in range(4):
        rows_ref[level, 8:80, :] = fine_ref[level]
        rows_ref[level, 7:8, :] = up_ref[level]
        rows_ref[level, 80:81, :] = down_ref[level]
        total = taps_ref[:, 0:1] * rows_ref[level, pl.ds(7, 36, stride=2), :]
        for t in range(1, 4):
            total = total + taps_ref[:, t : t + 1] * rows_ref[level, pl.ds(7 + t, 36, stride=2), :]
        part = jnp.dot(total, local, precision=HIGHEST, preferred_element_type=F32)
        for e in range(2):
            k = 2 * level + e
            all_ref[10 * k : 10 * k + 8, :] = part[16 * e : 16 * e + 8] + pltpu.roll(
                part[16 * e + 8 : 16 * e + 16], 64, 1
            )
            all_ref[10 * k + 8 : 10 * k + 10, :] = part[32 + 2 * e : 34 + 2 * e]
    for p in range(8):
        k = m ^ ORDER[p]
        block = all_ref[pl.ds(k * 10, 10), :]
        out, q = (keep_ref, p) if p < 4 else (send_ref, p - 4)
        out[8 * q : 8 * q + 8, :] = block[0:8]
        out[32 + 2 * q : 34 + 2 * q, :] = block[8:10]


def fine_part(m, fine, up, down, taps, weights):
    shape = jax.ShapeDtypeStruct((40, 128), F32)
    return pl.pallas_call(
        fine_kernel,
        out_shape=(shape, shape),
        in_specs=[pl.BlockSpec(memory_space=pltpu.SMEM)] + [pl.BlockSpec(memory_space=pltpu.VMEM)] * 5,
        out_specs=(pl.BlockSpec(memory_space=pltpu.VMEM),) * 2,
        scratch_shapes=[pltpu.VMEM((4, 88, 96), F32), pltpu.VMEM((80, 128), F32)],
        compiler_params=pltpu.CompilerParams(vmem_limit_bytes=16 * 2**20),
        cost_estimate=pl.CostEstimate(flops=4_000_000, bytes_accessed=1_500_000, transcendentals=0),
        name="fine",
    )(m, fine, up, down, taps, weights)


def merged(keep, recv, count):
    diff = keep[0] - recv[0]
    return keep[0] + recv[0], keep[1] + recv[1] + diff * diff * (0.5 / count)


def factor_kernel(count, m_ref, ka_ref, ra_ref, kb_ref, rb_ref, ik_ref, ir_ref, out_ref, wide_ref):
    m = m_ref[0]
    prior_total, prior_square = merged((ka_ref[0], ka_ref[1]), (ra_ref[0], ra_ref[1]), count // 2)
    post_total, post_square = merged(
        (kb_ref[0], kb_ref[1]), (rb_ref[:CHUNK], rb_ref[CHUNK : 2 * CHUNK]), count // 2
    )
    prior_mean = prior_total / count
    post_mean = post_total / count
    prior_spread = jnp.sqrt(prior_square / (count - 1) + 1e-06)
    post_spread = jnp.sqrt(post_square / (count - 1) + 1e-06)
    factor = 1.0 + 0.9 * (prior_spread - post_spread) / post_spread
    base = prior_mean - factor * post_mean
    wide = jnp.zeros((24, 384), F32)
    lane = lax.broadcasted_iota(jnp.int32, (24, 384), 1)
    for s in range(8):
        ref, q, at = (ik_ref, s, 0) if s < 4 else (ir_ref, s - 4, 0)
        tile = ref[8 * q : 8 * q + 8, :]
        rest = ref[32 + 2 * q : 34 + 2 * q, :]
        rows = jnp.concatenate([tile, pltpu.roll(tile, 64, 1), rest, jnp.zeros((6, 128), F32)], axis=0)
        rows = jnp.concatenate([rows, jnp.zeros((24, 256), F32)], axis=1)
        rows = jnp.where(lane < 50, rows, 0.0)
        wide = wide + pltpu.roll(rows, lax.rem(48 * (m ^ s) + 383, 384), 1)
    out_ref[0] = factor
    for rt in range(2):
        for ct in range(3):
            at = (3 * rt + ct) * 8
            out_ref[1, at : at + 8, :] = base[at : at + 8] + wide[8 * rt : 8 * rt + 8, 128 * ct : 128 * ct + 128]
    for ct in range(3):
        at = 48 + 2 * ct
        out_ref[1, at : at + 2, :] = base[at : at + 2] + wide[16:18, 128 * ct : 128 * ct + 128]
    out_ref[1, 54:56, :] = base[54:56]


def factor_part(count, m, *args):
    return pl.pallas_call(
        functools.partial(factor_kernel, count),
        out_shape=jax.ShapeDtypeStruct((2, CHUNK, 128), F32),
        in_specs=[pl.BlockSpec(memory_space=pltpu.SMEM)] + [pl.BlockSpec(memory_space=pltpu.VMEM)] * 6,
        out_specs=pl.BlockSpec(memory_space=pltpu.VMEM),
        scratch_shapes=[pltpu.VMEM((24, 384), F32)],
        cost_estimate=pl.CostEstimate(flops=1_000_000, bytes_accessed=400_000, transcendentals=20_000),
        name="factor",
    )(m, *args)


def output_kernel(m_ref, near_ref, far_ref, x_ref, out_ref, all_ref, full_ref):
    m = m_ref[0]

    @pl.when(pl.program_id(0) == 0)
    def _():
        for p in range(8):
            at = pl.multiple_of((m ^ ORDER[p]) * CHUNK, 8)
            ref, q = (near_ref, p * CHUNK) if p < 4 else (far_ref, (p - 4) * CHUNK)
            for which in range(2):
                all_ref[which, pl.ds(at, CHUNK), :] = ref[which, q : q + CHUNK, :]
        for which in range(2):
            for k in range(8):
                level, e = k // 2, k % 2
                base = k * CHUNK
                for rt in range(2):
                    for ct in range(3):
                        at = base + (3 * rt + ct) * 8
                        row = 16 * e + 8 * rt
                        full_ref[which, level, row : row + 8, 128 * ct : 128 * ct + 128] = all_ref[
                            which, at : at + 8, :
                        ]
                for ct in range(3):
                    at = base + 48 + 2 * ct
                    full_ref[which, level, 32 + 2 * e : 34 + 2 * e, 128 * ct : 128 * ct + 128] = all_ref[
                        which, at : at + 2, :
                    ]

    for level in range(4):
        factor = full_ref[0, level]
        base = full_ref[1, level]
        for i in range(x_ref.shape[0]):
            out_ref[i, level] = (base + factor * x_ref[i, level].astype(F32)).astype(jnp.bfloat16)


def output(m, near, far, x):
    members = x.shape[0]
    step = 2
    block = pl.BlockSpec((step, 4, 36, 384), lambda i: (i, 0, 0, 0))
    whole = pl.BlockSpec((2, 4 * CHUNK, 128), lambda i: (0, 0, 0))
    return pl.pallas_call(
        output_kernel,
        grid=(members // step,),
        out_shape=jax.ShapeDtypeStruct(x.shape, jnp.bfloat16),
        in_specs=[pl.BlockSpec(memory_space=pltpu.SMEM), whole, whole, block],
        out_specs=block,
        scratch_shapes=[pltpu.VMEM((2, 8 * CHUNK, 128), F32), pltpu.VMEM((2, 4, 36, 384), F32)],
        compiler_params=pltpu.CompilerParams(vmem_limit_bytes=16 * 2**20),
        cost_estimate=pl.CostEstimate(flops=2_000_000, bytes_accessed=3_000_000, transcendentals=0),
        name="output",
    )(m, near, far, x)


def on_device(fine_increment, row_taps, col_weights, prior, posterior):
    count = prior.shape[0] * lax.axis_size("mem")
    hor = lax.axis_size("hor")
    m = lax.axis_index("mem").astype(jnp.int32).reshape(1)

    def swap(x, distance):
        return lax.ppermute(x, "mem", [(i, i ^ distance) for i in range(8)])

    half, quarter = 2 * CHUNK, CHUNK
    keep_a, send_a = stats(m, prior)
    recv_a = swap(send_a, 1)
    keep_b, send_b = stats(m, posterior)
    recv_b = swap(send_b, 1)

    last = fine_increment[:, -1:, :]
    first = fine_increment[:, :1, :]
    up = lax.ppermute(last, "hor", [(i, i + 1) for i in range(hor - 1)])
    down = lax.ppermute(first, "hor", [(i + 1, i) for i in range(hor - 1)])
    inc_keep, inc_send = fine_part(m, fine_increment, up, down, row_taps.T, col_weights)
    inc_recv = swap(inc_send, 1)

    total, square = merged(keep_a, recv_a, count // 8)
    a = jnp.stack([total, square])
    keep_a, send_a = a[:, :half], a[:, half:]
    recv_a = swap(send_a, 2)

    total, square = merged(keep_b, recv_b, count // 8)
    keep_b = jnp.stack([total[:half], square[:half]])
    send = jnp.concatenate(
        [total[half:], square[half:], inc_keep[16:32], inc_recv[16:32], inc_keep[36:40], inc_recv[36:40]]
    )
    inc_keep = jnp.concatenate([inc_keep[:16], inc_recv[:16], inc_keep[32:36], inc_recv[32:36]])
    recv = swap(send, 2)
    recv_b = recv[: 2 * half].reshape(2, half, 128)
    inc_recv = recv[2 * half :]

    total, square = merged(keep_a, recv_a, count // 4)
    a = jnp.stack([total, square])
    keep_a, send_a = a[:, :quarter], a[:, quarter:]
    recv_a = swap(send_a, 4)

    total, square = merged(keep_b, recv_b, count // 4)
    keep_b = jnp.stack([total[:quarter], square[:quarter]])

    def of(position):
        tiles = [x[16 * s + 8 * position : 16 * s + 8 * position + 8] for x in (inc_keep, inc_recv) for s in range(2)]
        rests = [
            x[32 + 4 * s + 2 * position : 34 + 4 * s + 2 * position] for x in (inc_keep, inc_recv) for s in range(2)
        ]
        return tiles + rests

    send = jnp.concatenate([total[quarter:], square[quarter:]] + of(1))
    inc_keep = jnp.concatenate(of(0))
    recv = swap(send, 4)
    own = factor_part(count, m, keep_a, recv_a, keep_b, recv[: 2 * quarter], inc_keep, recv[2 * quarter :])

    near = jnp.concatenate([own, swap(own, 4)], axis=1)
    near = jnp.concatenate([near, swap(near, 2)], axis=1)
    far = swap(near, 1)
    return output(m, near, far, posterior)


def solution(mesh):
    return jax.shard_map(
        on_device,
        mesh=mesh,
        in_specs=(
            P(None, "hor", "mem"),
            P(None, "hor"),
            P(),
            P("mem", None, "hor", None),
            P("mem", None, "hor", None),
        ),
        out_specs=P("mem", None, "hor", None),
        check_vma=False,
    )
```

```python
import functools

import jax
import jax.numpy as jnp
from jax import lax
from jax.experimental import pallas as pl
from jax.experimental.layout import Layout, with_layout_constraint
from jax.experimental.pallas import tpu as pltpu
from jax.sharding import PartitionSpec as P

ROWS = 54
HALF = 2 * ROWS
STATS = 4 * ROWS
ORDER = (0, 4, 2, 6, 1, 5, 3, 7)
INC = 40
EDGE = 4
GATHER = HALF + EDGE
F32 = jnp.float32
HIGHEST = lax.Precision.HIGHEST
VMEM = pl.BlockSpec(memory_space=pltpu.VMEM)
SMEM = pl.BlockSpec(memory_space=pltpu.SMEM)


def call(kernel, name, ids, args, out, scratch=(), mib=4, flops=200_000, after=()):
    many = isinstance(out, tuple)
    moved = sum(a.size * a.dtype.itemsize for a in args) + sum(
        o.size * o.dtype.itemsize for o in (out if many else (out,))
    )
    count = len(args)

    def body(ids, *refs):
        kernel(ids, *refs[:count], *refs[count + len(after) :])

    return pl.pallas_call(
        body,
        out_shape=out,
        in_specs=[SMEM] + [VMEM] * count + [pl.BlockSpec(memory_space=pl.ANY)] * len(after),
        out_specs=(VMEM,) * len(out) if many else VMEM,
        scratch_shapes=list(scratch),
        compiler_params=pltpu.CompilerParams(vmem_limit_bytes=mib * 2**20),
        cost_estimate=pl.CostEstimate(flops=flops, bytes_accessed=moved, transcendentals=0),
        name=name,
    )(ids, *args, *after)


def rows_of(*counts):
    shapes = tuple(jax.ShapeDtypeStruct((count, 128), F32) for count in counts)
    return shapes if len(shapes) > 1 else shapes[0]


def stats_kernel(ids, prior, post, keep, send, full, block):
    step = 144
    for which, ref in enumerate((prior, post)):
        members = ref.shape[0]
        for at in range(0, 432, step):
            total = ref[0, at : at + step, :].astype(F32)
            for i in range(1, members):
                total = total + ref[i, at : at + step, :].astype(F32)
            mean = total / members
            square = jnp.zeros_like(total)
            for i in range(members):
                dev = ref[i, at : at + step, :].astype(F32) - mean
                square = square + dev * dev
            full[which, at : at + step, :] = total
            full[2 + which, at : at + step, :] = square
    for k in range(8):
        for j in range(4):
            at = k * STATS + j * ROWS
            block[at : at + ROWS, :] = full[j, pl.ds(4 * ROWS * (k >> 2) + (k & 3), ROWS, stride=4), :]
    for p in range(8):
        at = pl.multiple_of((ids[0] ^ ORDER[p]) * STATS, 8)
        out, to = (keep, p * STATS) if p < 4 else (send, (p - 4) * STATS)
        out[to : to + STATS, :] = block[pl.ds(at, STATS), :]


def local_weights(weights, device):
    own = weights[pl.ds(pl.multiple_of(device * 96, 32), 96), :]
    return pltpu.roll(own, lax.rem(385 - 48 * device, 384), 1)[:, :128]


def column(taps, t):
    size = taps.shape[1]
    diagonal = lax.broadcasted_iota(jnp.int32, (size, size), 0) == lax.broadcasted_iota(jnp.int32, (size, size), 1)
    return jnp.sum(jnp.where(diagonal, taps[t : t + 1, :], 0.0), axis=1, keepdims=True)


def fine_kernel(ids, fine, near, taps, weights, keep, send, rows, block):
    odd = ids[1] & 1
    local = local_weights(weights, ids[0])
    other = near[...]
    up = jnp.where(odd == 1, other, 0.0)
    down = jnp.where(odd == 1, 0.0, other)
    weight = [column(taps, t) for t in range(4)]
    for level in range(4):
        rows[8:80, :] = fine[level]
        rows[7:8, :] = up[level : level + 1]
        rows[80:81, :] = down[level : level + 1]
        total = weight[0] * rows[pl.ds(7, 36, stride=2), :]
        for t in range(1, 4):
            total = total + weight[t] * rows[pl.ds(7 + t, 36, stride=2), :]
        part = jnp.dot(total, local, precision=HIGHEST, preferred_element_type=F32)
        for e in range(2):
            at, row = 16 * (level + 4 * e), 18 * e
            block[at : at + 8, :] = part[row : row + 8] + pltpu.roll(part[row + 8 : row + 16], 64, 1)
            block[at + 8 : at + 9, :] = part[row + 16 : row + 17] + pltpu.roll(part[row + 17 : row + 18], 64, 1)
    for p in range(8):
        at = pl.multiple_of((ids[0] ^ ORDER[p]) * 16, 8)
        out, q = (keep, p) if p < 4 else (send, p - 4)
        out[8 * q : 8 * q + 8, :] = block[pl.ds(at, 8), :]
        out[32 + q : 33 + q, :] = block[pl.ds(at + 8, 8), :][0:1]
    for out in (keep, send):
        out[36:40, :] = jnp.zeros((4, 128), F32)


def merged(a, at, b, bt, count):
    one, two = a[at : at + HALF, :], b[bt : bt + HALF, :]
    diff = one - two
    squares = a[at + HALF : at + STATS, :] + b[bt + HALF : bt + STATS, :]
    return one + two, squares + diff * diff * (0.5 / count)


def merge_kernel(count, ids, keep, recv, *refs):
    *inc, keep_out, send_out = refs
    chunks = keep_out.shape[0] // STATS
    for p in range(2 * chunks):
        out, to = (keep_out, p * STATS) if p < chunks else (send_out, (p - chunks) * STATS)
        total, square = merged(keep, p * STATS, recv, p * STATS, count)
        out[to : to + HALF, :] = total
        out[to + HALF : to + STATS, :] = square
    old = 2 * chunks * STATS
    pairs = [(inc[0], 0), (inc[1], 0)] if inc else [(keep, old), (recv, old)]
    each = 4 // chunks // 2
    for half, out in enumerate((keep_out, send_out)):
        to = chunks * STATS
        for i, (ref, at) in enumerate(pairs):
            for s in range(each):
                for q in range(chunks):
                    new = (i * each + s) * chunks + q
                    old_place = s * 2 * chunks + half * chunks + q
                    out[to + 8 * new : to + 8 * new + 8, :] = ref[at + 8 * old_place : at + 8 * old_place + 8, :]
                    out[to + 32 + new : to + 33 + new, :] = ref[at + 32 + old_place : at + 33 + old_place, :]
        out[to + 36 : to + 40, :] = jnp.zeros((4, 128), F32)


def placed(ref, device):
    lane = lax.broadcasted_iota(jnp.int32, (18, 128), 1)
    wide = jnp.zeros((18, 384), F32)
    for s in range(4):
        most = ref[STATS + 8 * s : STATS + 8 * s + 8, :]
        rest = ref[STATS + 32 + s : STATS + 33 + s, :]
        share = jnp.concatenate([most, pltpu.roll(most, 64, 1), rest, pltpu.roll(rest, 64, 1)], axis=0)
        share = jnp.where(lane < 50, share, 0.0)
        share = jnp.concatenate([share, jnp.zeros((18, 256), F32)], axis=1)
        wide = wide + pltpu.roll(share, lax.rem(48 * (device ^ s) + 383, 384), 1)
    return wide


def own_kernel(ids, mine, out):
    out[...] = placed(mine, ids[0])


def edge_kernel(ids, late, taps, weights, out):
    tap = jnp.where(ids[1] & 1 == 1, taps[3:4, 35:36], taps[0:1, 0:1])
    out[...] = jnp.dot(
        late[...] * tap, local_weights(weights, ids[0] ^ ids[2]), precision=HIGHEST, preferred_element_type=F32
    )


def factor_kernel(count, ids, mine, recv, own, edge, out, scratch):
    total, square = merged(mine, 0, recv, 0, count // 2)
    mean = total / count
    spread = jnp.sqrt(square / (count - 1) + 1e-06)
    prior_spread, post_spread = spread[0:ROWS], spread[ROWS:HALF]
    factor = 1.0 + 0.9 * (prior_spread - post_spread) / post_spread
    wide = own[...] + placed(recv, ids[0] ^ 4)
    for ct in range(3):
        scratch[pl.ds(ct, 18, stride=3), :] = wide[:, 128 * ct : 128 * ct + 128]
    out[0:ROWS, :] = factor
    out[ROWS:HALF, :] = mean[0:ROWS] - factor * mean[ROWS:HALF] + scratch[...]
    out[HALF:GATHER, :] = edge[...]


def join_kernel(ids, a, b, out):
    size = a.shape[0]
    out[0:size, :] = a[...]
    out[size : 2 * size, :] = b[...]


def output_kernel(ids, near, far, post, out, block, factor, base):
    lane = lax.broadcasted_iota(jnp.int32, (EDGE, 128), 1)
    edge = jnp.zeros((EDGE, 384), F32)
    for p in range(8):
        ref, at = (near, p * GATHER) if p < 4 else (far, (p - 4) * GATHER)
        chunk = ids[0] ^ ORDER[p]
        block[pl.ds(pl.multiple_of(chunk * GATHER, 8), GATHER), :] = ref[at : at + GATHER, :]
        share = jnp.where(lane < 50, ref[at + HALF : at + GATHER, :], 0.0)
        share = jnp.concatenate([share, jnp.zeros((EDGE, 256), F32)], axis=1)
        edge = edge + pltpu.roll(share, lax.rem(48 * (chunk ^ ids[2]) + 383, 384), 1)
    for k in range(8):
        at = k * GATHER
        to = pl.ds(4 * ROWS * (k >> 2) + (k & 3), ROWS, stride=4)
        factor[to, :] = block[at : at + ROWS, :]
        base[to, :] = block[at + ROWS : at + HALF, :]
    odd = ids[1] & 1
    for ct in range(3):
        share = edge[:, 128 * ct : 128 * ct + 128]
        for at, part in ((0, jnp.where(odd == 1, 0.0, share)), (420, jnp.where(odd == 1, share, 0.0))):
            at = at + 4 * ct
            base[at : at + 4, :] = base[at : at + 4, :] + part
    step = 144
    for at in range(0, 432, step):
        scale = factor[at : at + step, :]
        shift = base[at : at + step, :]
        for i in range(post.shape[0]):
            out[i, at : at + step, :] = (shift + scale * post[i, at : at + step, :].astype(F32)).astype(jnp.bfloat16)


def viewed(x):
    members = x.shape[0]
    x = with_layout_constraint(x.reshape(members, 4, 36, 3, 128), Layout(major_to_minor=(0, 2, 3, 1, 4)))
    return x.transpose(0, 2, 3, 1, 4).reshape(members, 432, 128)


def on_device(fine_increment, row_taps, col_weights, prior, posterior):
    mem, hor = lax.axis_size("mem"), lax.axis_size("hor")
    share = prior.shape[0]
    count = share * mem
    m, h = lax.axis_index("mem"), lax.axis_index("hor")
    middle = hor // 2
    apart = jnp.where((h == middle - 1) | (h == middle), 4, 0)
    ids = jnp.stack([m, h, apart]).astype(jnp.int32)

    def swap(x, distance):
        return lax.ppermute(x, "mem", [(i, i ^ distance) for i in range(mem)])

    def swap_rows(x, first, far=None):
        pairs = [(i, i + 1) for i in range(first, hor - 1, 2)]
        pairs = pairs + [(j, i) for i, j in pairs]
        return lax.ppermute(
            x,
            ("mem", "hor"),
            [
                (i * hor + a, (i ^ (4 if a + b == 2 * middle - 1 and far else 0)) * hor + b)
                for i in range(mem)
                for a, b in pairs
            ],
        )

    prior, posterior = viewed(prior), viewed(posterior)
    last, first = fine_increment[:, -1, :], fine_increment[:, 0, :]
    odd = h % 2 == 1

    keep, send = call(
        stats_kernel,
        "stats",
        ids,
        (prior, posterior),
        rows_of(4 * STATS, 4 * STATS),
        [pltpu.VMEM((4, 432, 128), F32), pltpu.VMEM((8 * STATS, 128), F32)],
        mib=10,
        flops=8_000_000,
    )
    recv = swap(send, 1)
    now = swap_rows(jnp.where(odd, first, last), 0)
    inc_keep, inc_send = call(
        fine_kernel,
        "fine",
        ids,
        (fine_increment, now, row_taps, col_weights),
        rows_of(INC, INC),
        [pltpu.VMEM((88, 96), F32), pltpu.VMEM((128, 128), F32)],
        flops=4_000_000,
    )
    inc_recv = swap(inc_send, 1)
    keep, send = call(
        functools.partial(merge_kernel, share),
        "merge1",
        ids,
        (keep, recv, inc_keep, inc_recv),
        rows_of(2 * STATS + INC, 2 * STATS + INC),
    )
    recv = swap(send, 2)
    late, _ = lax.optimization_barrier((jnp.where(odd, last, first), keep))
    late = swap_rows(late, 1, True)
    edge = call(
        edge_kernel, "edge", ids, (late, row_taps, col_weights), rows_of(EDGE)
    )
    keep, send = call(
        functools.partial(merge_kernel, 2 * share), "merge2", ids, (keep, recv), rows_of(STATS + INC, STATS + INC)
    )
    recv = swap(send, 4)
    own = call(own_kernel, "own", ids, (keep,), jax.ShapeDtypeStruct((18, 384), F32))
    near = call(
        functools.partial(factor_kernel, count),
        "factor",
        ids,
        (keep, recv, own, edge),
        rows_of(GATHER),
        [pltpu.VMEM((ROWS, 128), F32)],
    )
    for distance in (4, 2):
        near = call(join_kernel, "join", ids, (near, swap(near, distance)), rows_of(2 * near.shape[0]))
    far = swap(near, 1)
    out = call(
        output_kernel,
        "output",
        ids,
        (near, far, posterior),
        jax.ShapeDtypeStruct(posterior.shape, jnp.bfloat16),
        [pltpu.VMEM((8 * GATHER, 128), F32)] + [pltpu.VMEM((432, 128), F32)] * 2,
        mib=10,
        flops=2_000_000,
    )
    out = out.reshape(share, 36, 3, 4, 128).transpose(0, 1, 3, 2, 4)
    return out.reshape(share, 36, 4, 384).transpose(0, 2, 1, 3)


def solution(mesh):
    return jax.shard_map(
        on_device,
        mesh=mesh,
        in_specs=(
            P(None, "hor", "mem"),
            P(None, "hor"),
            P(),
            P("mem", None, "hor", None),
            P("mem", None, "hor", None),
        ),
        out_specs=P("mem", None, "hor", None),
        check_vma=False,
    )
```

```python
import functools

import jax
import jax.numpy as jnp
from jax import lax
from jax.experimental import pallas as pl
from jax.experimental.layout import Layout, with_layout_constraint
from jax.experimental.pallas import tpu as pltpu
from jax.sharding import PartitionSpec as P

ROWS = 54
HALF = 2 * ROWS
STATS = 4 * ROWS
SENT = 2 * STATS + 24
KEPT = STATS + 40
EDGE = 4
GATHER = HALF + EDGE
F32 = jnp.float32
HIGHEST = lax.Precision.HIGHEST
VMEM = pl.BlockSpec(memory_space=pltpu.VMEM)
SMEM = pl.BlockSpec(memory_space=pltpu.SMEM)


def call(kernel, name, ids, args, out, scratch=(), mib=4, flops=200_000, specs=None):
    many = isinstance(out, tuple)
    moved = sum(a.size * a.dtype.itemsize for a in args) + sum(
        o.size * o.dtype.itemsize for o in (out if many else (out,))
    )
    return pl.pallas_call(
        kernel,
        out_shape=out,
        in_specs=[SMEM] + (specs or [VMEM] * len(args)),
        out_specs=(VMEM,) * len(out) if many else VMEM,
        scratch_shapes=list(scratch),
        compiler_params=pltpu.CompilerParams(vmem_limit_bytes=mib * 2**20),
        cost_estimate=pl.CostEstimate(flops=flops, bytes_accessed=moved, transcendentals=0),
        name=name,
    )(ids, *args)


def rows_of(*counts):
    shapes = tuple(jax.ShapeDtypeStruct((count, 128), F32) for count in counts)
    return shapes if len(shapes) > 1 else shapes[0]


def local_weights(own, device):
    return pltpu.roll(own, lax.rem(385 - 48 * device, 384), 1)[:, :128]


def column(taps, t):
    size = taps.shape[1]
    diagonal = lax.broadcasted_iota(jnp.int32, (size, size), 0) == lax.broadcasted_iota(jnp.int32, (size, size), 1)
    return jnp.sum(jnp.where(diagonal, taps[t : t + 1, :], 0.0), axis=1, keepdims=True)


def first_kernel(ids, prior, post, fine, taps, weights, *refs):
    outs, (members, rows, tap, weight, sems, full, block) = refs[:4], refs[4:]
    m = ids[0]
    copies = [
        pltpu.make_async_copy(src, dst, sems.at[i])
        for i, (src, dst) in enumerate(
            (
                (fine, rows.at[:, pl.ds(8, 72), :]),
                (weights.at[pl.ds(pl.multiple_of(96 * m, 32), 96), :], weight),
                (taps, tap),
                (prior, members.at[0]),
                (post, members.at[1]),
            )
        )
    ]
    for copy in copies:
        copy.start()
    for copy in copies[:3]:
        copy.wait()
    local = local_weights(weight[...], m)
    columns = [column(tap, t) for t in range(4)]
    for level in range(4):
        rows[level, 0:8, :] = jnp.zeros((8, 96), F32)
        rows[level, 80:88, :] = jnp.zeros((8, 96), F32)
        total = columns[0] * rows[level, pl.ds(7, 36, stride=2), :]
        for t in range(1, 4):
            total = total + columns[t] * rows[level, pl.ds(7 + t, 36, stride=2), :]
        part = jnp.dot(total, local, precision=HIGHEST, preferred_element_type=F32)
        for e in range(2):
            at, row = (level + 4 * e) * SENT // 2 + STATS, 18 * e
            block[at : at + 8, :] = part[row : row + 8] + pltpu.roll(part[row + 8 : row + 16], 64, 1)
            block[at + 8 : at + 9, :] = part[row + 16 : row + 17] + pltpu.roll(part[row + 17 : row + 18], 64, 1)
    step = 144
    for which in range(2):
        copies[3 + which].wait()
        count = members.shape[1]
        for at in range(0, 432, step):
            total = members[which, 0, at : at + step, :].astype(F32)
            for i in range(1, count):
                total = total + members[which, i, at : at + step, :].astype(F32)
            mean = total / count
            square = jnp.zeros_like(total)
            for i in range(count):
                dev = members[which, i, at : at + step, :].astype(F32) - mean
                square = square + dev * dev
            full[which, at : at + step, :] = total
            full[2 + which, at : at + step, :] = square
    for k in range(8):
        for j in range(4):
            at = k * SENT // 2 + j * ROWS
            block[at : at + ROWS, :] = full[j, pl.ds(4 * ROWS * (k >> 2) + (k & 3), ROWS, stride=4), :]
    for d, out in enumerate(outs):
        for i in range(2):
            at = pl.multiple_of((m ^ d ^ (4 * i)) * (SENT // 2), 4)
            out[i * STATS : (i + 1) * STATS, :] = block[pl.ds(at, STATS), :]
            out[2 * STATS + 8 * i : 2 * STATS + 8 * i + 8, :] = block[pl.ds(at + STATS, 8), :]
            out[2 * STATS + 16 + i : 2 * STATS + 17 + i, :] = block[pl.ds(at + STATS + 8, 1), :]
        out[2 * STATS + 18 : SENT, :] = jnp.zeros((6, 128), F32)


def merge_kernel(members, ids, *refs):
    edge, keep, send, edge_out = refs[4:]
    edge_out[...] = edge[...]
    for i, out in enumerate((keep, send)):
        at = i * STATS
        sums = [ref[at : at + HALF, :] for ref in refs[:4]]
        total = (sums[0] + sums[1]) + (sums[2] + sums[3])
        mean = total / (4 * members)
        square = jnp.zeros_like(total)
        for one, ref in zip(sums, refs[:4]):
            dev = one / members - mean
            square = square + (ref[at + HALF : at + STATS, :] + members * (dev * dev))
        out[0:HALF, :] = total
        out[HALF:STATS, :] = square
        for s, ref in enumerate(refs[:4]):
            share = 2 * STATS + 8 * i
            out[STATS + 8 * s : STATS + 8 * s + 8, :] = ref[share : share + 8, :]
            share = 2 * STATS + 16 + i
            out[STATS + 32 + s : STATS + 33 + s, :] = ref[share : share + 1, :]
        out[STATS + 36 : KEPT, :] = jnp.zeros((4, 128), F32)


def placed(share, source):
    lane = lax.broadcasted_iota(jnp.int32, share.shape, 1)
    share = jnp.where(lane < 50, share, 0.0)
    share = jnp.concatenate([share, jnp.zeros((share.shape[0], 256), F32)], axis=1)
    return pltpu.roll(share, lax.rem(48 * source + 383, 384), 1)


def placed_chunk(ref, device):
    wide = jnp.zeros((18, 384), F32)
    for s in range(4):
        most = ref[STATS + 8 * s : STATS + 8 * s + 8, :]
        rest = ref[STATS + 32 + s : STATS + 33 + s, :]
        share = jnp.concatenate([most, pltpu.roll(most, 64, 1), rest, pltpu.roll(rest, 64, 1)], axis=0)
        wide = wide + placed(share, device ^ s)
    return wide


def own_kernel(ids, mine, out):
    out[...] = placed_chunk(mine, ids[0])


def edge_kernel(ids, near, late, taps, weights, out):
    odd = ids[1] & 1
    above, below = taps[0:1, 0:1], taps[3:4, 35:36]
    share = []
    for rows, tap, source in (
        (near, jnp.where(odd == 1, above, below), ids[0]),
        (late, jnp.where(odd == 1, below, above), ids[0] ^ ids[2]),
    ):
        local = local_weights(weights[pl.ds(pl.multiple_of(96 * source, 32), 96), :], source)
        share.append(jnp.dot(rows[...] * tap, local, precision=HIGHEST, preferred_element_type=F32))
    out[...] = share[0] + pltpu.roll(share[1], 64, 1)


def merged(a, b, count):
    one, two = a[0:HALF, :], b[0:HALF, :]
    diff = one - two
    squares = a[HALF:STATS, :] + b[HALF:STATS, :]
    return one + two, squares + diff * diff * (0.5 / count)


def factor_kernel(count, ids, mine, recv, own, edge, out, scratch):
    total, square = merged(mine, recv, count // 2)
    mean = total / count
    spread = jnp.sqrt(square / (count - 1) + 1e-06)
    prior_spread, post_spread = spread[0:ROWS], spread[ROWS:HALF]
    factor = 1.0 + 0.9 * (prior_spread - post_spread) / post_spread
    wide = own[...] + placed_chunk(recv, ids[0] ^ 4)
    for ct in range(3):
        scratch[pl.ds(ct, 18, stride=3), :] = wide[:, 128 * ct : 128 * ct + 128]
    out[0:ROWS, :] = factor
    out[ROWS:HALF, :] = mean[0:ROWS] - factor * mean[ROWS:HALF] + scratch[...]
    out[HALF:GATHER, :] = edge[...]


def join_kernel(ids, a, b, out):
    size = a.shape[0]
    out[0:size, :] = a[...]
    out[size : 2 * size, :] = b[...]


def output_kernel(ids, own, one, two, three, post, out, block, factor, base):
    near = jnp.zeros((EDGE, 384), F32)
    late = near
    for d, ref in enumerate((own, one, two, three)):
        for i in range(2):
            at = i * GATHER
            chunk = ids[0] ^ d ^ (4 * i)
            block[pl.ds(pl.multiple_of(chunk * GATHER, 8), GATHER), :] = ref[at : at + GATHER, :]
            share = ref[at + HALF : at + GATHER, :]
            near = near + placed(share, chunk)
            late = late + placed(pltpu.roll(share, 64, 1), chunk ^ ids[2])
    for k in range(8):
        at = k * GATHER
        to = pl.ds(4 * ROWS * (k >> 2) + (k & 3), ROWS, stride=4)
        factor[to, :] = block[at : at + ROWS, :]
        base[to, :] = block[at + ROWS : at + HALF, :]
    odd = ids[1] & 1
    above = jnp.where(odd == 1, near, late)
    below = jnp.where(odd == 1, late, near)
    for ct in range(3):
        for at, part in ((4 * ct, above), (420 + 4 * ct, below)):
            base[at : at + 4, :] = base[at : at + 4, :] + part[:, 128 * ct : 128 * ct + 128]
    step = 144
    for at in range(0, 432, step):
        scale = factor[at : at + step, :]
        shift = base[at : at + step, :]
        for i in range(post.shape[0]):
            out[i, at : at + step, :] = (shift + scale * post[i, at : at + step, :].astype(F32)).astype(jnp.bfloat16)


def viewed(x):
    members = x.shape[0]
    x = with_layout_constraint(x.reshape(members, 4, 36, 3, 128), Layout(major_to_minor=(0, 2, 3, 1, 4)))
    return x.transpose(0, 2, 3, 1, 4).reshape(members, 432, 128)


def on_device(fine_increment, row_taps, col_weights, prior, posterior):
    mem, hor = lax.axis_size("mem"), lax.axis_size("hor")
    share = prior.shape[0]
    count = share * mem
    m, h = lax.axis_index("mem"), lax.axis_index("hor")
    middle = hor // 2
    apart = jnp.where((h == middle - 1) | (h == middle), 4, 0)
    ids = jnp.stack([m, h, apart]).astype(jnp.int32)

    def swap(x, distance):
        return lax.ppermute(x, "mem", [(i, i ^ distance) for i in range(mem)])

    def swap_rows(x, first, far=None):
        pairs = [(i, i + 1) for i in range(first, hor - 1, 2)]
        pairs = pairs + [(j, i) for i, j in pairs]
        return lax.ppermute(
            x,
            ("mem", "hor"),
            [
                (i * hor + a, (i ^ (4 if a + b == 2 * middle - 1 and far else 0)) * hor + b)
                for i in range(mem)
                for a, b in pairs
            ],
        )

    prior, posterior = viewed(prior), viewed(posterior)
    last, first = fine_increment[:, -1, :], fine_increment[:, 0, :]
    odd = h % 2 == 1

    own, *sent = call(
        first_kernel,
        "first",
        ids,
        (prior, posterior, fine_increment, row_taps, col_weights),
        rows_of(SENT, SENT, SENT, SENT),
        [
            pltpu.VMEM((2, share, 432, 128), jnp.bfloat16),
            pltpu.VMEM((4, 88, 96), F32),
            pltpu.VMEM((4, 36), F32),
            pltpu.VMEM((96, 384), F32),
            pltpu.SemaphoreType.DMA((5,)),
            pltpu.VMEM((4, 432, 128), F32),
            pltpu.VMEM((4 * SENT, 128), F32),
        ],
        mib=60,
        flops=12_000_000,
        specs=[pl.BlockSpec(memory_space=pltpu.HBM)] * 5,
    )
    got = [swap(x, d) for d, x in enumerate(sent, 1)]
    near = swap_rows(jnp.where(odd, first, last), 0)
    late = swap_rows(jnp.where(odd, last, first), 1, True)
    edge = call(edge_kernel, "edge", ids, (near, late, row_taps, col_weights), rows_of(EDGE))
    keep, send, edge = call(
        functools.partial(merge_kernel, share), "merge", ids, [own, *got, edge], rows_of(KEPT, KEPT, EDGE)
    )
    recv = swap(send, 4)
    own = call(own_kernel, "own", ids, (keep,), jax.ShapeDtypeStruct((18, 384), F32))
    near = call(
        functools.partial(factor_kernel, count),
        "factor",
        ids,
        (keep, recv, own, edge),
        rows_of(GATHER),
        [pltpu.VMEM((ROWS, 128), F32)],
    )
    near = call(join_kernel, "join", ids, (near, swap(near, 4)), rows_of(2 * GATHER))
    gathered = [near] + [swap(near, distance) for distance in (1, 2, 3)]
    out = call(
        output_kernel,
        "output",
        ids,
        (*gathered, posterior),
        jax.ShapeDtypeStruct(posterior.shape, jnp.bfloat16),
        [pltpu.VMEM((8 * GATHER, 128), F32)] + [pltpu.VMEM((432, 128), F32)] * 2,
        mib=10,
        flops=2_000_000,
    )
    out = out.reshape(share, 36, 3, 4, 128).transpose(0, 1, 3, 2, 4)
    return out.reshape(share, 36, 4, 384).transpose(0, 2, 1, 3)


def solution(mesh):
    return jax.shard_map(
        on_device,
        mesh=mesh,
        in_specs=(
            P(None, "hor", "mem"),
            P(None, "hor"),
            P(),
            P("mem", None, "hor", None),
            P("mem", None, "hor", None),
        ),
        out_specs=P("mem", None, "hor", None),
        check_vma=False,
    )
```

```python
import functools

import jax
import jax.numpy as jnp
from jax import lax
from jax.experimental import pallas as pl
from jax.experimental.layout import Layout, with_layout_constraint
from jax.experimental.pallas import tpu as pltpu
from jax.sharding import PartitionSpec as P

ROWS = 54
HALF = 2 * ROWS
STATS = 4 * ROWS
SENT = STATS + 16
PAIR = STATS + 24
KEPT = STATS + 40
EDGE = 4
GATHER = HALF + EDGE
F32 = jnp.float32
HIGHEST = lax.Precision.HIGHEST
VMEM = pl.BlockSpec(memory_space=pltpu.VMEM)
SMEM = pl.BlockSpec(memory_space=pltpu.SMEM)


def call(kernel, name, ids, args, out, scratch=(), mib=4, flops=200_000, specs=None, outs=None, aliases=None):
    many = isinstance(out, tuple)
    moved = sum(a.size * a.dtype.itemsize for a in args) + sum(
        o.size * o.dtype.itemsize for o in (out if many else (out,))
    )
    return pl.pallas_call(
        kernel,
        out_shape=out,
        in_specs=[SMEM] + (specs or [VMEM] * len(args)),
        out_specs=tuple(outs or (VMEM,) * len(out)) if many else VMEM,
        scratch_shapes=list(scratch),
        input_output_aliases=aliases or {},
        compiler_params=pltpu.CompilerParams(vmem_limit_bytes=mib * 2**20),
        cost_estimate=pl.CostEstimate(flops=flops, bytes_accessed=moved, transcendentals=0),
        name=name,
    )(ids, *args)


def rows_of(*counts):
    shapes = tuple(jax.ShapeDtypeStruct((count, 128), F32) for count in counts)
    return shapes if len(shapes) > 1 else shapes[0]


def local_weights(own, device):
    return pltpu.roll(own, lax.rem(385 - 48 * device, 384), 1)[:, :128]


def column(taps, t):
    size = taps.shape[1]
    diagonal = lax.broadcasted_iota(jnp.int32, (size, size), 0) == lax.broadcasted_iota(jnp.int32, (size, size), 1)
    return jnp.sum(jnp.where(diagonal, taps[t : t + 1, :], 0.0), axis=1, keepdims=True)


def first_kernel(ids, prior, post, fine, taps, weights, *refs):
    outs, (near, late, edge), (members, rows, tap, weight, sems, full, block) = refs[:5], refs[5:8], refs[8:]
    m = ids[0]
    copies = [
        pltpu.make_async_copy(src, dst, sems.at[i])
        for i, (src, dst) in enumerate(
            (
                (fine, rows.at[:, pl.ds(8, 72), :]),
                (weights.at[pl.ds(pl.multiple_of(96 * m, 32), 96), :], weight.at[0]),
                (weights.at[pl.ds(pl.multiple_of(96 * (m ^ ids[2]), 32), 96), :], weight.at[1]),
                (taps, tap),
                (prior, members.at[0]),
                (post, members.at[1]),
            )
        )
    ]
    for copy in copies:
        copy.start()
    for copy in copies[:4]:
        copy.wait()
    odd = ids[1] & 1
    for level in range(4):
        first, last = rows[level, 8:9, :], rows[level, 79:80, :]
        near[level : level + 1, :] = jnp.where(odd == 1, first, last)
        late[level : level + 1, :] = jnp.where(odd == 1, last, first)
    local = local_weights(weight[0], m)
    above, below = tap[0:1, 0:1], tap[3:4, 35:36]
    edge[0] = local * jnp.where(odd == 1, above, below)
    edge[1] = local_weights(weight[1], m ^ ids[2]) * jnp.where(odd == 1, below, above)
    columns = [column(tap, t) for t in range(4)]
    for level in range(4):
        rows[level, 0:8, :] = jnp.zeros((8, 96), F32)
        rows[level, 80:88, :] = jnp.zeros((8, 96), F32)
        total = columns[0] * rows[level, pl.ds(7, 36, stride=2), :]
        for t in range(1, 4):
            total = total + columns[t] * rows[level, pl.ds(7 + t, 36, stride=2), :]
        part = jnp.dot(total, local, precision=HIGHEST, preferred_element_type=F32)
        for e in range(2):
            at, row = (level + 4 * e) * SENT + STATS, 18 * e
            block[at : at + 8, :] = part[row : row + 8] + pltpu.roll(part[row + 8 : row + 16], 64, 1)
            block[at + 8 : at + 9, :] = part[row + 16 : row + 17] + pltpu.roll(part[row + 17 : row + 18], 64, 1)
            block[at + 9 : at + 16, :] = jnp.zeros((7, 128), F32)
    step = 144
    for which in range(2):
        copies[4 + which].wait()
        count = members.shape[1]
        for at in range(0, 432, step):
            total = members[which, 0, at : at + step, :].astype(F32)
            for i in range(1, count):
                total = total + members[which, i, at : at + step, :].astype(F32)
            mean = total / count
            square = jnp.zeros_like(total)
            for i in range(count):
                dev = members[which, i, at : at + step, :].astype(F32) - mean
                square = square + dev * dev
            full[which, at : at + step, :] = total
            full[2 + which, at : at + step, :] = square
    for k in range(8):
        for j in range(4):
            at = k * SENT + j * ROWS
            block[at : at + ROWS, :] = full[j, pl.ds(4 * ROWS * (k >> 2) + (k & 3), ROWS, stride=4), :]
    for out, distances in zip(outs, ((4,), (0, 2), (5, 1, 3), (6,), (7,))):
        for i, d in enumerate(distances):
            out[i * SENT : (i + 1) * SENT, :] = block[pl.ds(pl.multiple_of((m ^ d) * SENT, 8), SENT), :]


def merge(members, refs, out):
    sums = [ref[0:HALF, :] for ref in refs]
    total = (sums[0] + sums[1]) + (sums[2] + sums[3])
    mean = total / (4 * members)
    square = jnp.zeros_like(total)
    for one, ref in zip(sums, refs):
        dev = one / members - mean
        square = square + (ref[HALF:STATS, :] + members * (dev * dev))
    out[0:HALF, :] = total
    out[HALF:STATS, :] = square
    for s, ref in enumerate(refs):
        out[STATS + 8 * s : STATS + 8 * s + 8, :] = ref[STATS : STATS + 8, :]
        out[STATS + 32 + s : STATS + 33 + s, :] = ref[STATS + 8 : STATS + 9, :]
    out[STATS + 36 : KEPT, :] = jnp.zeros((4, 128), F32)


def merged(a, at, b, bt, count):
    one, two = a[at : at + HALF, :], b[bt : bt + HALF, :]
    diff = one - two
    squares = a[at + HALF : at + STATS, :] + b[bt + HALF : bt + STATS, :]
    return one + two, squares + diff * diff * (0.5 / count)


def merge_pair_kernel(members, ids, mine, recv, near, own, on):
    for i, out in enumerate((own, on)):
        at, bt = i * SENT, (1 + i) * SENT
        total, square = merged(mine, at, recv, bt, members)
        out[0:HALF, :] = total
        out[HALF:STATS, :] = square
        for s, (ref, to) in enumerate(((mine, at + STATS), (recv, bt + STATS))):
            out[STATS + 8 * s : STATS + 8 * s + 8, :] = ref[to : to + 8, :]
            out[STATS + 16 + s : STATS + 17 + s, :] = ref[to + 8 : to + 9, :]
        out[STATS + 18 : PAIR, :] = jnp.zeros((6, 128), F32)


def merge_on_kernel(members, ids, *refs):
    merge(members, refs[:4], refs[6])


def merge_own_kernel(members, ids, mine, recv, near, late, weights, keep, wide, edge):
    total, square = merged(mine, 0, recv, 0, 2 * members)
    keep[0:HALF, :] = total
    keep[HALF:STATS, :] = square
    for s, ref in enumerate((mine, recv)):
        keep[STATS + 16 * s : STATS + 16 * s + 16, :] = ref[STATS : STATS + 16, :]
        keep[STATS + 32 + 2 * s : STATS + 34 + 2 * s, :] = ref[STATS + 16 : STATS + 18, :]
    keep[STATS + 36 : KEPT, :] = jnp.zeros((4, 128), F32)
    wide[...] = placed_chunk(keep, ids[0])
    shares = [
        jnp.dot(rows[...], weights[i], precision=HIGHEST, preferred_element_type=F32)
        for i, rows in enumerate((near, late))
    ]
    edge[...] = shares[0] + pltpu.roll(shares[1], 64, 1)


def placed(share, source):
    lane = lax.broadcasted_iota(jnp.int32, share.shape, 1)
    share = jnp.where(lane < 50, share, 0.0)
    share = jnp.concatenate([share, jnp.zeros((share.shape[0], 256), F32)], axis=1)
    return pltpu.roll(share, lax.rem(48 * source + 383, 384), 1)


def placed_chunk(ref, device):
    wide = jnp.zeros((18, 384), F32)
    for s in range(4):
        most = ref[STATS + 8 * s : STATS + 8 * s + 8, :]
        rest = ref[STATS + 32 + s : STATS + 33 + s, :]
        share = jnp.concatenate([most, pltpu.roll(most, 64, 1), rest, pltpu.roll(rest, 64, 1)], axis=0)
        wide = wide + placed(share, device ^ s)
    return wide


def factor_kernel(count, ids, mine, recv, own, edge, out, scratch):
    total, square = merged(mine, 0, recv, 0, count // 2)
    mean = total / count
    spread = jnp.sqrt(square / (count - 1) + 1e-06)
    prior_spread, post_spread = spread[0:ROWS], spread[ROWS:HALF]
    factor = 1.0 + 0.9 * (prior_spread - post_spread) / post_spread
    wide = own[...] + placed_chunk(recv, ids[0] ^ 4)
    for ct in range(3):
        scratch[pl.ds(ct, 18, stride=3), :] = wide[:, 128 * ct : 128 * ct + 128]
    out[0:ROWS, :] = factor
    out[ROWS:HALF, :] = mean[0:ROWS] - factor * mean[ROWS:HALF] + scratch[...]
    out[HALF:GATHER, :] = edge[...]


def join_kernel(ids, a, b, out):
    size = a.shape[0]
    out[0:size, :] = a[...]
    out[size : 2 * size, :] = b[...]


def output_kernel(ids, own, one, two, three, post, out, block, factor, base):
    near = jnp.zeros((EDGE, 384), F32)
    late = near
    for d, ref in enumerate((own, one, two, three)):
        for i in range(2):
            at = i * GATHER
            chunk = ids[0] ^ d ^ (4 * i)
            block[pl.ds(pl.multiple_of(chunk * GATHER, 8), GATHER), :] = ref[at : at + GATHER, :]
            share = ref[at + HALF : at + GATHER, :]
            near = near + placed(share, chunk)
            late = late + placed(pltpu.roll(share, 64, 1), chunk ^ ids[2])
    for k in range(8):
        at = k * GATHER
        to = pl.ds(4 * ROWS * (k >> 2) + (k & 3), ROWS, stride=4)
        factor[to, :] = block[at : at + ROWS, :]
        base[to, :] = block[at + ROWS : at + HALF, :]
    odd = ids[1] & 1
    above = jnp.where(odd == 1, near, late)
    below = jnp.where(odd == 1, late, near)
    for ct in range(3):
        for at, part in ((4 * ct, above), (420 + 4 * ct, below)):
            base[at : at + 4, :] = base[at : at + 4, :] + part[:, 128 * ct : 128 * ct + 128]
    step = 144
    for at in range(0, 432, step):
        scale = factor[at : at + step, :]
        shift = base[at : at + step, :]
        for i in range(post.shape[0]):
            out[i, at : at + step, :] = (shift + scale * post[i, at : at + step, :].astype(F32)).astype(jnp.bfloat16)


def viewed(x):
    members = x.shape[0]
    x = with_layout_constraint(x.reshape(members, 4, 36, 3, 128), Layout(major_to_minor=(0, 2, 3, 1, 4)))
    return x.transpose(0, 2, 3, 1, 4).reshape(members, 432, 128)


def on_device(fine_increment, row_taps, col_weights, prior, posterior):
    mem, hor = lax.axis_size("mem"), lax.axis_size("hor")
    share = prior.shape[0]
    count = share * mem
    m, h = lax.axis_index("mem"), lax.axis_index("hor")
    middle = hor // 2
    apart = jnp.where((h == middle - 1) | (h == middle), 4, 0)
    ids = jnp.stack([m, h, apart]).astype(jnp.int32)

    def swap(x, distance):
        return lax.ppermute(x, "mem", [(i, i ^ distance) for i in range(mem)])

    def swap_rows(x, first, far=None):
        pairs = [(i, i + 1) for i in range(first, hor - 1, 2)]
        pairs = pairs + [(j, i) for i, j in pairs]
        return lax.ppermute(
            x,
            ("mem", "hor"),
            [
                (i * hor + a, (i ^ (4 if a + b == 2 * middle - 1 and far else 0)) * hor + b)
                for i in range(mem)
                for a, b in pairs
            ],
        )

    prior, posterior = viewed(prior), viewed(posterior)

    row = jax.ShapeDtypeStruct((4, 96), F32)
    on, own, *sent, near, late, weights = call(
        first_kernel,
        "first",
        ids,
        (prior, posterior, fine_increment, row_taps, col_weights),
        rows_of(SENT, 2 * SENT, 3 * SENT, SENT, SENT) + (row, row, jax.ShapeDtypeStruct((2, 96, 128), F32)),
        [
            pltpu.VMEM((2, share, 432, 128), jnp.bfloat16),
            pltpu.VMEM((4, 88, 96), F32),
            pltpu.VMEM((4, 36), F32),
            pltpu.VMEM((2, 96, 384), F32),
            pltpu.SemaphoreType.DMA((6,)),
            pltpu.VMEM((4, 432, 128), F32),
            pltpu.VMEM((8 * SENT, 128), F32),
        ],
        mib=52,
        flops=12_000_000,
        specs=[pl.BlockSpec(memory_space=pltpu.HBM)] * 5,
    )
    got = [swap(x, d) for d, x in enumerate(sent, 1)]
    near = swap_rows(near, 0)
    own, pair = call(
        functools.partial(merge_pair_kernel, share), "merge_pair", ids, (own, got[0], near), rows_of(PAIR, PAIR)
    )
    anywhere = [pl.BlockSpec(memory_space=pl.ANY)]
    send, late = call(
        functools.partial(merge_on_kernel, share),
        "merge_on",
        ids,
        (on, *got, pair, late),
        (rows_of(KEPT), row),
        specs=[VMEM] * 4 + anywhere * 2,
        outs=[VMEM] + anywhere,
        aliases={6: 1},
    )
    recv = swap(send, 4)
    keep, own, edge = call(
        functools.partial(merge_own_kernel, share),
        "merge_own",
        ids,
        (own, swap(pair, 2), near, swap_rows(late, 1, True), weights),
        (rows_of(KEPT), jax.ShapeDtypeStruct((18, 384), F32), rows_of(EDGE)),
    )
    near = call(
        functools.partial(factor_kernel, count),
        "factor",
        ids,
        (keep, recv, own, edge),
        rows_of(GATHER),
        [pltpu.VMEM((ROWS, 128), F32)],
    )
    near = call(join_kernel, "join", ids, (near, swap(near, 4)), rows_of(2 * GATHER))
    gathered = [near] + [swap(near, distance) for distance in (1, 2, 3)]
    out = call(
        output_kernel,
        "output",
        ids,
        (*gathered, posterior),
        jax.ShapeDtypeStruct(posterior.shape, jnp.bfloat16),
        [pltpu.VMEM((8 * GATHER, 128), F32)] + [pltpu.VMEM((432, 128), F32)] * 2,
        mib=10,
        flops=2_000_000,
    )
    out = out.reshape(share, 36, 3, 4, 128).transpose(0, 1, 3, 2, 4)
    return out.reshape(share, 36, 4, 384).transpose(0, 2, 1, 3)


def solution(mesh):
    return jax.shard_map(
        on_device,
        mesh=mesh,
        in_specs=(
            P(None, "hor", "mem"),
            P(None, "hor"),
            P(),
            P("mem", None, "hor", None),
            P("mem", None, "hor", None),
        ),
        out_specs=P("mem", None, "hor", None),
        check_vma=False,
    )
```

```python
import functools

import jax
import jax.numpy as jnp
from jax import lax
from jax.experimental import pallas as pl
from jax.experimental.layout import Layout, with_layout_constraint
from jax.experimental.pallas import tpu as pltpu
from jax.sharding import PartitionSpec as P

ROWS = 54
HALF = 2 * ROWS
STATS = 4 * ROWS
SENT = STATS + 16
PAIR = STATS + 24
KEPT = STATS + 40
EDGE = 4
GATHER = HALF + EDGE
F32 = jnp.float32
HIGHEST = lax.Precision.HIGHEST
VMEM = pl.BlockSpec(memory_space=pltpu.VMEM)
SMEM = pl.BlockSpec(memory_space=pltpu.SMEM)


def call(kernel, name, ids, args, out, scratch=(), mib=4, flops=200_000, specs=None, outs=None, aliases=None):
    many = isinstance(out, tuple)
    moved = sum(a.size * a.dtype.itemsize for a in args) + sum(
        o.size * o.dtype.itemsize for o in (out if many else (out,))
    )
    return pl.pallas_call(
        kernel,
        out_shape=out,
        in_specs=[SMEM] + (specs or [VMEM] * len(args)),
        out_specs=tuple(outs or (VMEM,) * len(out)) if many else VMEM,
        scratch_shapes=list(scratch),
        input_output_aliases=aliases or {},
        compiler_params=pltpu.CompilerParams(vmem_limit_bytes=mib * 2**20),
        cost_estimate=pl.CostEstimate(flops=flops, bytes_accessed=moved, transcendentals=0),
        name=name,
    )(ids, *args)


def rows_of(*counts):
    shapes = tuple(jax.ShapeDtypeStruct((count, 128), F32) for count in counts)
    return shapes if len(shapes) > 1 else shapes[0]


def local_weights(own, device):
    return pltpu.roll(own, lax.rem(385 - 48 * device, 384), 1)[:, :128]


def column(taps, t):
    size = taps.shape[1]
    diagonal = lax.broadcasted_iota(jnp.int32, (size, size), 0) == lax.broadcasted_iota(jnp.int32, (size, size), 1)
    return jnp.sum(jnp.where(diagonal, taps[t : t + 1, :], 0.0), axis=1, keepdims=True)


def first_kernel(ids, prior, post, fine, taps, weights, *refs):
    outs, (near, late, edge), (members, rows, tap, weight, sems, full, block) = refs[:5], refs[5:8], refs[8:]
    m = ids[0]
    copies = [
        pltpu.make_async_copy(src, dst, sems.at[i])
        for i, (src, dst) in enumerate(
            (
                (fine, rows.at[:, pl.ds(8, 72), :]),
                (weights.at[pl.ds(pl.multiple_of(96 * m, 32), 96), :], weight.at[0]),
                (weights.at[pl.ds(pl.multiple_of(96 * (m ^ ids[2]), 32), 96), :], weight.at[1]),
                (taps, tap),
                (prior, members.at[0]),
                (post, members.at[1]),
            )
        )
    ]
    for copy in copies:
        copy.start()
    for copy in copies[:4]:
        copy.wait()
    odd = ids[1] & 1
    for level in range(4):
        first, last = rows[level, 8:9, :], rows[level, 79:80, :]
        near[level : level + 1, :] = jnp.where(odd == 1, first, last)
        late[level : level + 1, :] = jnp.where(odd == 1, last, first)
    local = local_weights(weight[0], m)
    above, below = tap[0:1, 0:1], tap[3:4, 35:36]
    edge[0] = local * jnp.where(odd == 1, above, below)
    edge[1] = local_weights(weight[1], m ^ ids[2]) * jnp.where(odd == 1, below, above)
    columns = [column(tap, t) for t in range(4)]
    for level in range(4):
        rows[level, 0:8, :] = jnp.zeros((8, 96), F32)
        rows[level, 80:88, :] = jnp.zeros((8, 96), F32)
        total = columns[0] * rows[level, pl.ds(7, 36, stride=2), :]
        for t in range(1, 4):
            total = total + columns[t] * rows[level, pl.ds(7 + t, 36, stride=2), :]
        part = jnp.dot(total, local, precision=HIGHEST, preferred_element_type=F32)
        for e in range(2):
            at, row = (level + 4 * e) * SENT + STATS, 18 * e
            block[at : at + 8, :] = part[row : row + 8] + pltpu.roll(part[row + 8 : row + 16], 64, 1)
            block[at + 8 : at + 9, :] = part[row + 16 : row + 17] + pltpu.roll(part[row + 17 : row + 18], 64, 1)
            block[at + 9 : at + 16, :] = jnp.zeros((7, 128), F32)
    step = 144
    for which in range(2):
        copies[4 + which].wait()
        count = members.shape[1]
        for at in range(0, 432, step):
            total = members[which, 0, at : at + step, :].astype(F32)
            for i in range(1, count):
                total = total + members[which, i, at : at + step, :].astype(F32)
            mean = total / count
            square = jnp.zeros_like(total)
            for i in range(count):
                dev = members[which, i, at : at + step, :].astype(F32) - mean
                square = square + dev * dev
            full[which, at : at + step, :] = total
            full[2 + which, at : at + step, :] = square
    for k in range(8):
        for j in range(4):
            at = k * SENT + j * ROWS
            block[at : at + ROWS, :] = full[j, pl.ds(4 * ROWS * (k >> 2) + (k & 3), ROWS, stride=4), :]
    for out, distances in zip(outs, ((4,), (0, 2), (5, 1, 3), (6,), (7,))):
        for i, d in enumerate(distances):
            out[i * SENT : (i + 1) * SENT, :] = block[pl.ds(pl.multiple_of((m ^ d) * SENT, 8), SENT), :]


def merge(members, refs, out):
    sums = [ref[0:HALF, :] for ref in refs]
    total = (sums[0] + sums[1]) + (sums[2] + sums[3])
    mean = total / (4 * members)
    square = jnp.zeros_like(total)
    for one, ref in zip(sums, refs):
        dev = one / members - mean
        square = square + (ref[HALF:STATS, :] + members * (dev * dev))
    out[0:HALF, :] = total
    out[HALF:STATS, :] = square
    for s, ref in enumerate(refs):
        out[STATS + 8 * s : STATS + 8 * s + 8, :] = ref[STATS : STATS + 8, :]
        out[STATS + 32 + s : STATS + 33 + s, :] = ref[STATS + 8 : STATS + 9, :]
    out[STATS + 36 : KEPT, :] = jnp.zeros((4, 128), F32)


def merged(a, at, b, bt, count):
    one, two = a[at : at + HALF, :], b[bt : bt + HALF, :]
    diff = one - two
    squares = a[at + HALF : at + STATS, :] + b[bt + HALF : bt + STATS, :]
    return one + two, squares + diff * diff * (0.5 / count)


def merge_pair_kernel(members, ids, mine, recv, near, own, on):
    for i, out in enumerate((own, on)):
        at, bt = i * SENT, (1 + i) * SENT
        total, square = merged(mine, at, recv, bt, members)
        out[0:HALF, :] = total
        out[HALF:STATS, :] = square
        for s, (ref, to) in enumerate(((mine, at + STATS), (recv, bt + STATS))):
            out[STATS + 8 * s : STATS + 8 * s + 8, :] = ref[to : to + 8, :]
            out[STATS + 16 + s : STATS + 17 + s, :] = ref[to + 8 : to + 9, :]
        out[STATS + 18 : PAIR, :] = jnp.zeros((6, 128), F32)


def merge_on_kernel(members, ids, *refs):
    merge(members, refs[3::-1], refs[6])


def placed(share, source):
    lane = lax.broadcasted_iota(jnp.int32, share.shape, 1)
    share = jnp.where(lane < 50, share, 0.0)
    share = jnp.concatenate([share, jnp.zeros((share.shape[0], 256), F32)], axis=1)
    return pltpu.roll(share, lax.rem(48 * source + 383, 384), 1)


def placed_chunk(ref, device, count):
    wide = jnp.zeros((18, 384), F32)
    for s in range(count):
        most = ref[STATS + 8 * s : STATS + 8 * s + 8, :]
        rest = ref[STATS + 8 * count + s : STATS + 8 * count + s + 1, :]
        share = jnp.concatenate([most, pltpu.roll(most, 64, 1), rest, pltpu.roll(rest, 64, 1)], axis=0)
        wide = wide + placed(share, device ^ s)
    return wide


def put_together(one, two, count):
    diff = one[0] - two[0]
    return one[0] + two[0], one[1] + two[1] + diff * diff * (0.5 / count)


def factor_kernel(count, ids, mine, two, recv, near, late, weights, out, scratch):
    pair, more, rest = ((ref[0:HALF, :], ref[HALF:STATS, :]) for ref in (mine, two, recv))
    total, square = put_together(put_together(pair, more, count // 4), rest, count // 2)
    mean = total / count
    spread = jnp.sqrt(square / (count - 1) + 1e-06)
    prior_spread, post_spread = spread[0:ROWS], spread[ROWS:HALF]
    factor = 1.0 + 0.9 * (prior_spread - post_spread) / post_spread
    wide = placed_chunk(mine, ids[0], 2) + placed_chunk(two, ids[0] ^ 2, 2) + placed_chunk(recv, ids[0] ^ 4, 4)
    for ct in range(3):
        scratch[pl.ds(ct, 18, stride=3), :] = wide[:, 128 * ct : 128 * ct + 128]
    out[0:ROWS, :] = factor
    out[ROWS:HALF, :] = mean[0:ROWS] - factor * mean[ROWS:HALF] + scratch[...]
    shares = [
        jnp.dot(rows[...], weights[i], precision=HIGHEST, preferred_element_type=F32)
        for i, rows in enumerate((near, late))
    ]
    out[HALF:GATHER, :] = shares[0] + pltpu.roll(shares[1], 64, 1)


def join_kernel(ids, a, b, out):
    size = a.shape[0]
    out[0:size, :] = a[...]
    out[size : 2 * size, :] = b[...]


def output_kernel(ids, own, one, two, three, post, out, block, factor, base):
    near = jnp.zeros((EDGE, 384), F32)
    late = near
    for d, ref in enumerate((own, one, two, three)):
        for i in range(2):
            at = i * GATHER
            chunk = ids[0] ^ d ^ (4 * i)
            block[pl.ds(pl.multiple_of(chunk * GATHER, 8), GATHER), :] = ref[at : at + GATHER, :]
            share = ref[at + HALF : at + GATHER, :]
            near = near + placed(share, chunk)
            late = late + placed(pltpu.roll(share, 64, 1), chunk ^ ids[2])
    for k in range(8):
        at = k * GATHER
        to = pl.ds(4 * ROWS * (k >> 2) + (k & 3), ROWS, stride=4)
        factor[to, :] = block[at : at + ROWS, :]
        base[to, :] = block[at + ROWS : at + HALF, :]
    odd = ids[1] & 1
    above = jnp.where(odd == 1, near, late)
    below = jnp.where(odd == 1, late, near)
    for ct in range(3):
        for at, part in ((4 * ct, above), (420 + 4 * ct, below)):
            base[at : at + 4, :] = base[at : at + 4, :] + part[:, 128 * ct : 128 * ct + 128]
    step = 144
    for at in range(0, 432, step):
        scale = factor[at : at + step, :]
        shift = base[at : at + step, :]
        for i in range(post.shape[0]):
            out[i, at : at + step, :] = (shift + scale * post[i, at : at + step, :].astype(F32)).astype(jnp.bfloat16)


def viewed(x):
    members = x.shape[0]
    x = with_layout_constraint(x.reshape(members, 4, 36, 3, 128), Layout(major_to_minor=(0, 2, 3, 1, 4)))
    return x.transpose(0, 2, 3, 1, 4).reshape(members, 432, 128)


def on_device(fine_increment, row_taps, col_weights, prior, posterior):
    mem, hor = lax.axis_size("mem"), lax.axis_size("hor")
    share = prior.shape[0]
    count = share * mem
    m, h = lax.axis_index("mem"), lax.axis_index("hor")
    middle = hor // 2
    apart = jnp.where((h == middle - 1) | (h == middle), 4, 0)
    ids = jnp.stack([m, h, apart]).astype(jnp.int32)

    def swap(x, distance):
        return lax.ppermute(x, "mem", [(i, i ^ distance) for i in range(mem)])

    def swap_rows(x, first, far=None):
        pairs = [(i, i + 1) for i in range(first, hor - 1, 2)]
        pairs = pairs + [(j, i) for i, j in pairs]
        return lax.ppermute(
            x,
            ("mem", "hor"),
            [
                (i * hor + a, (i ^ (4 if a + b == 2 * middle - 1 and far else 0)) * hor + b)
                for i in range(mem)
                for a, b in pairs
            ],
        )

    prior, posterior = viewed(prior), viewed(posterior)

    row = jax.ShapeDtypeStruct((4, 96), F32)
    on, own, *sent, near, late, weights = call(
        first_kernel,
        "first",
        ids,
        (prior, posterior, fine_increment, row_taps, col_weights),
        rows_of(SENT, 2 * SENT, 3 * SENT, SENT, SENT) + (row, row, jax.ShapeDtypeStruct((2, 96, 128), F32)),
        [
            pltpu.VMEM((2, share, 432, 128), jnp.bfloat16),
            pltpu.VMEM((4, 88, 96), F32),
            pltpu.VMEM((4, 36), F32),
            pltpu.VMEM((2, 96, 384), F32),
            pltpu.SemaphoreType.DMA((6,)),
            pltpu.VMEM((4, 432, 128), F32),
            pltpu.VMEM((8 * SENT, 128), F32),
        ],
        mib=52,
        flops=12_000_000,
        specs=[pl.BlockSpec(memory_space=pltpu.HBM)] * 5,
    )
    got = [swap(x, d) for d, x in enumerate(sent, 1)]
    near = swap_rows(near, 0)
    own, pair = call(
        functools.partial(merge_pair_kernel, share), "merge_pair", ids, (own, got[0], near), rows_of(PAIR, PAIR)
    )
    anywhere = [pl.BlockSpec(memory_space=pl.ANY)]
    send, late = call(
        functools.partial(merge_on_kernel, share),
        "merge_on",
        ids,
        (*got[::-1], on, pair, late),
        (rows_of(KEPT), row),
        specs=[VMEM] * 4 + anywhere * 2,
        outs=[VMEM] + anywhere,
        aliases={6: 1},
    )
    recv = swap(send, 4)
    near = call(
        functools.partial(factor_kernel, count),
        "factor",
        ids,
        (own, swap(pair, 2), recv, near, swap_rows(late, 1, True), weights),
        rows_of(GATHER),
        [pltpu.VMEM((ROWS, 128), F32)],
    )
    near = call(join_kernel, "join", ids, (near, swap(near, 4)), rows_of(2 * GATHER))
    gathered = [near] + [swap(near, distance) for distance in (1, 2, 3)]
    out = call(
        output_kernel,
        "output",
        ids,
        (*gathered, posterior),
        jax.ShapeDtypeStruct(posterior.shape, jnp.bfloat16),
        [pltpu.VMEM((8 * GATHER, 128), F32)] + [pltpu.VMEM((432, 128), F32)] * 2,
        mib=10,
        flops=2_000_000,
    )
    out = out.reshape(share, 36, 3, 4, 128).transpose(0, 1, 3, 2, 4)
    return out.reshape(share, 36, 4, 384).transpose(0, 2, 1, 3)


def solution(mesh):
    return jax.shard_map(
        on_device,
        mesh=mesh,
        in_specs=(
            P(None, "hor", "mem"),
            P(None, "hor"),
            P(),
            P("mem", None, "hor", None),
            P("mem", None, "hor", None),
        ),
        out_specs=P("mem", None, "hor", None),
        check_vma=False,
    )
```

```python
import functools

import jax
import jax.numpy as jnp
from jax import lax
from jax.experimental import pallas as pl
from jax.experimental.layout import Layout, with_layout_constraint
from jax.experimental.pallas import tpu as pltpu
from jax.sharding import PartitionSpec as P

ROWS = 54
HALF = 2 * ROWS
STATS = 4 * ROWS
SENT = STATS + 16
PAIR = STATS + 24
KEPT = STATS + 40
EDGE = 4
GATHER = HALF + EDGE
F32 = jnp.float32
HIGHEST = lax.Precision.HIGHEST
VMEM = pl.BlockSpec(memory_space=pltpu.VMEM)
SMEM = pl.BlockSpec(memory_space=pltpu.SMEM)


def call(kernel, name, ids, args, out, scratch=(), mib=4, flops=200_000, specs=None, outs=None, aliases=None):
    many = isinstance(out, tuple)
    moved = sum(a.size * a.dtype.itemsize for a in args) + sum(
        o.size * o.dtype.itemsize for o in (out if many else (out,))
    )
    return pl.pallas_call(
        kernel,
        out_shape=out,
        in_specs=[SMEM] + (specs or [VMEM] * len(args)),
        out_specs=tuple(outs or (VMEM,) * len(out)) if many else VMEM,
        scratch_shapes=list(scratch),
        input_output_aliases=aliases or {},
        compiler_params=pltpu.CompilerParams(vmem_limit_bytes=mib * 2**20),
        cost_estimate=pl.CostEstimate(flops=flops, bytes_accessed=moved, transcendentals=0),
        name=name,
    )(ids, *args)


def rows_of(*counts):
    shapes = tuple(jax.ShapeDtypeStruct((count, 128), F32) for count in counts)
    return shapes if len(shapes) > 1 else shapes[0]


def local_weights(own, device):
    return pltpu.roll(own, lax.rem(385 - 48 * device, 384), 1)[:, :128]


def column(taps, t):
    size = taps.shape[1]
    diagonal = lax.broadcasted_iota(jnp.int32, (size, size), 0) == lax.broadcasted_iota(jnp.int32, (size, size), 1)
    return jnp.sum(jnp.where(diagonal, taps[t : t + 1, :], 0.0), axis=1, keepdims=True)


def first_kernel(ids, prior, post, packed, weights, *refs):
    outs, (near, late, edge), (members, rows, weight, sems, full, block) = refs[:5], refs[5:8], refs[8:]
    m = ids[0]
    copies = [
        pltpu.make_async_copy(src, dst, sems.at[i])
        for i, (src, dst) in enumerate(
            (
                (weights.at[pl.ds(pl.multiple_of(96 * m, 32), 96), :], weight.at[0]),
                (weights.at[pl.ds(pl.multiple_of(96 * (m ^ ids[2]), 32), 96), :], weight.at[1]),
                (prior, members.at[0]),
                (post, members.at[1]),
            )
        )
    ]
    for copy in copies:
        copy.start()
    for copy in copies[:2]:
        copy.wait()
    tap = jnp.concatenate([packed[t, 72:73, 0:36] for t in range(4)], axis=0)
    odd = ids[1] & 1
    for level in range(4):
        rows[level, 8:80, :] = packed[level, 0:72, 0:96]
        first, last = rows[level, 8:9, :], rows[level, 79:80, :]
        near[level : level + 1, :] = jnp.where(odd == 1, first, last)
        late[level : level + 1, :] = jnp.where(odd == 1, last, first)
    local = local_weights(weight[0], m)
    above, below = tap[0:1, 0:1], tap[3:4, 35:36]
    edge[0] = local * jnp.where(odd == 1, above, below)
    edge[1] = local_weights(weight[1], m ^ ids[2]) * jnp.where(odd == 1, below, above)
    columns = [column(tap, t) for t in range(4)]
    for level in range(4):
        rows[level, 0:8, :] = jnp.zeros((8, 96), F32)
        rows[level, 80:88, :] = jnp.zeros((8, 96), F32)
        total = columns[0] * rows[level, pl.ds(7, 36, stride=2), :]
        for t in range(1, 4):
            total = total + columns[t] * rows[level, pl.ds(7 + t, 36, stride=2), :]
        part = jnp.dot(total, local, precision=HIGHEST, preferred_element_type=F32)
        for e in range(2):
            at, row = (level + 4 * e) * SENT + STATS, 18 * e
            block[at : at + 8, :] = part[row : row + 8] + pltpu.roll(part[row + 8 : row + 16], 64, 1)
            block[at + 8 : at + 9, :] = part[row + 16 : row + 17] + pltpu.roll(part[row + 17 : row + 18], 64, 1)
            block[at + 9 : at + 16, :] = jnp.zeros((7, 128), F32)
    step = 16
    for which in range(2):
        copies[2 + which].wait()
        count = members.shape[1]
        for at in range(0, 432, step):
            values = [members[which, i, at : at + step, :].astype(F32) for i in range(count)]
            total = values[0]
            for value in values[1:]:
                total = total + value
            mean = total / count
            square = jnp.zeros_like(total)
            for value in values:
                dev = value - mean
                square = square + dev * dev
            full[which, at : at + step, :] = total
            full[2 + which, at : at + step, :] = square
    for k in range(8):
        for j in range(4):
            at = k * SENT + j * ROWS
            block[at : at + ROWS, :] = full[j, pl.ds(4 * ROWS * (k >> 2) + (k & 3), ROWS, stride=4), :]
    for out, distances in zip(outs, ((4,), (0, 2), (5, 1, 3), (6,), (7,))):
        for i, d in enumerate(distances):
            out[i * SENT : (i + 1) * SENT, :] = block[pl.ds(pl.multiple_of((m ^ d) * SENT, 8), SENT), :]


def merge(members, refs, out):
    sums = [ref[0:HALF, :] for ref in refs]
    total = (sums[0] + sums[1]) + (sums[2] + sums[3])
    mean = total / (4 * members)
    square = jnp.zeros_like(total)
    for one, ref in zip(sums, refs):
        dev = one / members - mean
        square = square + (ref[HALF:STATS, :] + members * (dev * dev))
    out[0:HALF, :] = total
    out[HALF:STATS, :] = square
    for s, ref in enumerate(refs):
        out[STATS + 8 * s : STATS + 8 * s + 8, :] = ref[STATS : STATS + 8, :]
        out[STATS + 32 + s : STATS + 33 + s, :] = ref[STATS + 8 : STATS + 9, :]
    out[STATS + 36 : KEPT, :] = jnp.zeros((4, 128), F32)


def merged(a, at, b, bt, count):
    one, two = a[at : at + HALF, :], b[bt : bt + HALF, :]
    diff = one - two
    squares = a[at + HALF : at + STATS, :] + b[bt + HALF : bt + STATS, :]
    return one + two, squares + diff * diff * (0.5 / count)


def merge_pair_kernel(members, ids, mine, recv, near, own, on):
    for i, out in enumerate((own, on)):
        at, bt = i * SENT, (1 + i) * SENT
        total, square = merged(mine, at, recv, bt, members)
        out[0:HALF, :] = total
        out[HALF:STATS, :] = square
        for s, (ref, to) in enumerate(((mine, at + STATS), (recv, bt + STATS))):
            out[STATS + 8 * s : STATS + 8 * s + 8, :] = ref[to : to + 8, :]
            out[STATS + 16 + s : STATS + 17 + s, :] = ref[to + 8 : to + 9, :]
        out[STATS + 18 : PAIR, :] = jnp.zeros((6, 128), F32)


def merge_on_kernel(members, ids, *refs):
    merge(members, refs[3::-1], refs[6])


def placed(share, source):
    lane = lax.broadcasted_iota(jnp.int32, share.shape, 1)
    share = jnp.where(lane < 50, share, 0.0)
    share = jnp.concatenate([share, jnp.zeros((share.shape[0], 256), F32)], axis=1)
    return pltpu.roll(share, lax.rem(48 * source + 383, 384), 1)


def placed_chunk(ref, device, count):
    wide = jnp.zeros((18, 384), F32)
    for s in range(count):
        most = ref[STATS + 8 * s : STATS + 8 * s + 8, :]
        rest = ref[STATS + 8 * count + s : STATS + 8 * count + s + 1, :]
        share = jnp.concatenate([most, pltpu.roll(most, 64, 1), rest, pltpu.roll(rest, 64, 1)], axis=0)
        wide = wide + placed(share, device ^ s)
    return wide


def put_together(one, two, count):
    diff = one[0] - two[0]
    return one[0] + two[0], one[1] + two[1] + diff * diff * (0.5 / count)


def factor_kernel(count, ids, mine, two, recv, near, late, weights, out, scratch):
    pair, more, rest = ((ref[0:HALF, :], ref[HALF:STATS, :]) for ref in (mine, two, recv))
    total, square = put_together(put_together(pair, more, count // 4), rest, count // 2)
    mean = total / count
    spread = jnp.sqrt(square / (count - 1) + 1e-06)
    prior_spread, post_spread = spread[0:ROWS], spread[ROWS:HALF]
    factor = 1.0 + 0.9 * (prior_spread - post_spread) / post_spread
    wide = placed_chunk(mine, ids[0], 2) + placed_chunk(two, ids[0] ^ 2, 2) + placed_chunk(recv, ids[0] ^ 4, 4)
    for ct in range(3):
        scratch[pl.ds(ct, 18, stride=3), :] = wide[:, 128 * ct : 128 * ct + 128]
    out[0:ROWS, :] = factor
    out[ROWS:HALF, :] = mean[0:ROWS] - factor * mean[ROWS:HALF] + scratch[...]
    shares = [
        jnp.dot(rows[...], weights[i], precision=HIGHEST, preferred_element_type=F32)
        for i, rows in enumerate((near, late))
    ]
    out[HALF:GATHER, :] = shares[0] + pltpu.roll(shares[1], 64, 1)


def join_kernel(ids, a, b, out):
    size = a.shape[0]
    out[0:size, :] = a[...]
    out[size : 2 * size, :] = b[...]


def output_kernel(ids, own, one, two, three, post, out, block, factor, base):
    near = jnp.zeros((EDGE, 384), F32)
    late = near
    for d, ref in enumerate((own, one, two, three)):
        for i in range(2):
            at = i * GATHER
            chunk = ids[0] ^ d ^ (4 * i)
            block[pl.ds(pl.multiple_of(chunk * GATHER, 8), GATHER), :] = ref[at : at + GATHER, :]
            share = ref[at + HALF : at + GATHER, :]
            near = near + placed(share, chunk)
            late = late + placed(pltpu.roll(share, 64, 1), chunk ^ ids[2])
    for k in range(8):
        at = k * GATHER
        to = pl.ds(4 * ROWS * (k >> 2) + (k & 3), ROWS, stride=4)
        factor[to, :] = block[at : at + ROWS, :]
        base[to, :] = block[at + ROWS : at + HALF, :]
    odd = ids[1] & 1
    above = jnp.where(odd == 1, near, late)
    below = jnp.where(odd == 1, late, near)
    for ct in range(3):
        for at, part in ((4 * ct, above), (420 + 4 * ct, below)):
            base[at : at + 4, :] = base[at : at + 4, :] + part[:, 128 * ct : 128 * ct + 128]
    step = 144
    for at in range(0, 432, step):
        scale = factor[at : at + step, :]
        shift = base[at : at + step, :]
        for i in range(post.shape[0]):
            out[i, at : at + step, :] = (shift + scale * post[i, at : at + step, :].astype(F32)).astype(jnp.bfloat16)


def viewed(x):
    members = x.shape[0]
    x = with_layout_constraint(x.reshape(members, 4, 36, 3, 128), Layout(major_to_minor=(0, 2, 3, 1, 4)))
    return x.transpose(0, 2, 3, 1, 4).reshape(members, 432, 128)


def on_device(fine_increment, row_taps, col_weights, prior, posterior):
    mem, hor = lax.axis_size("mem"), lax.axis_size("hor")
    share = prior.shape[0]
    count = share * mem
    m, h = lax.axis_index("mem"), lax.axis_index("hor")
    middle = hor // 2
    apart = jnp.where((h == middle - 1) | (h == middle), 4, 0)
    ids = jnp.stack([m, h, apart]).astype(jnp.int32)

    def swap(x, distance):
        return lax.ppermute(x, "mem", [(i, i ^ distance) for i in range(mem)])

    def swap_rows(x, first, far=None):
        pairs = [(i, i + 1) for i in range(first, hor - 1, 2)]
        pairs = pairs + [(j, i) for i, j in pairs]
        return lax.ppermute(
            x,
            ("mem", "hor"),
            [
                (i * hor + a, (i ^ (4 if a + b == 2 * middle - 1 and far else 0)) * hor + b)
                for i in range(mem)
                for a, b in pairs
            ],
        )

    prior, posterior = viewed(prior), viewed(posterior)

    row = jax.ShapeDtypeStruct((4, 96), F32)
    packed = jnp.pad(fine_increment, ((0, 0), (0, 8), (0, 32)))
    packed = packed + jnp.pad(row_taps[:, None, :], ((0, 0), (72, 7), (0, 92)))
    on, own, *sent, near, late, weights = call(
        first_kernel,
        "first",
        ids,
        (prior, posterior, packed, col_weights),
        rows_of(SENT, 2 * SENT, 3 * SENT, SENT, SENT) + (row, row, jax.ShapeDtypeStruct((2, 96, 128), F32)),
        [
            pltpu.VMEM((2, share, 432, 128), jnp.bfloat16),
            pltpu.VMEM((4, 88, 96), F32),
            pltpu.VMEM((2, 96, 384), F32),
            pltpu.SemaphoreType.DMA((4,)),
            pltpu.VMEM((4, 432, 128), F32),
            pltpu.VMEM((8 * SENT, 128), F32),
        ],
        mib=52,
        flops=12_000_000,
        specs=[pl.BlockSpec(memory_space=pltpu.HBM)] * 2 + [VMEM, pl.BlockSpec(memory_space=pltpu.HBM)],
    )
    got = [swap(x, d) for d, x in enumerate(sent, 1)]
    near = swap_rows(near, 0)
    own, pair = call(
        functools.partial(merge_pair_kernel, share), "merge_pair", ids, (own, got[0], near), rows_of(PAIR, PAIR)
    )
    anywhere = [pl.BlockSpec(memory_space=pl.ANY)]
    send, late = call(
        functools.partial(merge_on_kernel, share),
        "merge_on",
        ids,
        (*got[::-1], on, pair, late),
        (rows_of(KEPT), row),
        specs=[VMEM] * 4 + anywhere * 2,
        outs=[VMEM] + anywhere,
        aliases={6: 1},
    )
    recv = swap(send, 4)
    near = call(
        functools.partial(factor_kernel, count),
        "factor",
        ids,
        (own, swap(pair, 2), recv, near, swap_rows(late, 1, True), weights),
        rows_of(GATHER),
        [pltpu.VMEM((ROWS, 128), F32)],
    )
    near = call(join_kernel, "join", ids, (near, swap(near, 4)), rows_of(2 * GATHER))
    gathered = [near] + [swap(near, distance) for distance in (1, 2, 3)]
    out = call(
        output_kernel,
        "output",
        ids,
        (*gathered, posterior),
        jax.ShapeDtypeStruct(posterior.shape, jnp.bfloat16),
        [pltpu.VMEM((8 * GATHER, 128), F32)] + [pltpu.VMEM((432, 128), F32)] * 2,
        mib=10,
        flops=2_000_000,
    )
    out = out.reshape(share, 36, 3, 4, 128).transpose(0, 1, 3, 2, 4)
    return out.reshape(share, 36, 4, 384).transpose(0, 2, 1, 3)


def solution(mesh):
    return jax.shard_map(
        on_device,
        mesh=mesh,
        in_specs=(
            P(None, "hor", "mem"),
            P(None, "hor"),
            P(),
            P("mem", None, "hor", None),
            P("mem", None, "hor", None),
        ),
        out_specs=P("mem", None, "hor", None),
        check_vma=False,
    )
```

```python
import functools

import jax
import jax.numpy as jnp
from jax import lax
from jax.experimental import pallas as pl
from jax.experimental.layout import Layout, with_layout_constraint
from jax.experimental.pallas import tpu as pltpu
from jax.sharding import PartitionSpec as P

ROWS = 54
HALF = 2 * ROWS
STATS = 4 * ROWS
SENT = STATS + 16
PAIR = STATS + 24
KEPT = STATS + 40
EDGE = 4
GATHER = HALF + EDGE
F32 = jnp.float32
HIGHEST = lax.Precision.HIGHEST
VMEM = pl.BlockSpec(memory_space=pltpu.VMEM)
SMEM = pl.BlockSpec(memory_space=pltpu.SMEM)


def call(kernel, name, ids, args, out, scratch=(), mib=4, flops=200_000, specs=None, outs=None, aliases=None):
    many = isinstance(out, tuple)
    moved = sum(a.size * a.dtype.itemsize for a in args) + sum(
        o.size * o.dtype.itemsize for o in (out if many else (out,))
    )
    return pl.pallas_call(
        kernel,
        out_shape=out,
        in_specs=[SMEM] + (specs or [VMEM] * len(args)),
        out_specs=tuple(outs or (VMEM,) * len(out)) if many else (outs or VMEM),
        scratch_shapes=list(scratch),
        input_output_aliases=aliases or {},
        compiler_params=pltpu.CompilerParams(vmem_limit_bytes=mib * 2**20),
        cost_estimate=pl.CostEstimate(flops=flops, bytes_accessed=moved, transcendentals=0),
        name=name,
    )(ids, *args)


def rows_of(*counts):
    shapes = tuple(jax.ShapeDtypeStruct((count, 128), F32) for count in counts)
    return shapes if len(shapes) > 1 else shapes[0]


def local_weights(own, device):
    return pltpu.roll(own, lax.rem(385 - 48 * device, 384), 1)[:, :128]


def column(taps, t):
    size = taps.shape[1]
    diagonal = lax.broadcasted_iota(jnp.int32, (size, size), 0) == lax.broadcasted_iota(jnp.int32, (size, size), 1)
    return jnp.sum(jnp.where(diagonal, taps[t : t + 1, :], 0.0), axis=1, keepdims=True)


def first_kernel(ids, prior, post, packed, weights, *refs):
    outs, (near, late, edge), (members, rows, weight, sems, full, block) = refs[:5], refs[5:8], refs[8:]
    m = ids[0]
    copies = [
        pltpu.make_async_copy(src, dst, sems.at[i])
        for i, (src, dst) in enumerate(
            (
                (weights.at[pl.ds(pl.multiple_of(96 * m, 32), 96), :], weight.at[0]),
                (weights.at[pl.ds(pl.multiple_of(96 * (m ^ ids[2]), 32), 96), :], weight.at[1]),
                (prior, members.at[0]),
                (post, members.at[1]),
            )
        )
    ]
    for copy in copies:
        copy.start()
    for copy in copies[:2]:
        copy.wait()
    tap = jnp.concatenate([packed[t, 72:73, 0:36] for t in range(4)], axis=0)
    odd = ids[1] & 1
    for level in range(4):
        rows[level, 8:80, :] = packed[level, 0:72, 0:96]
        first, last = rows[level, 8:9, :], rows[level, 79:80, :]
        near[level : level + 1, :] = jnp.where(odd == 1, first, last)
        late[level : level + 1, :] = jnp.where(odd == 1, last, first)
    local = local_weights(weight[0], m)
    above, below = tap[0:1, 0:1], tap[3:4, 35:36]
    edge[0] = local * jnp.where(odd == 1, above, below)
    edge[1] = local_weights(weight[1], m ^ ids[2]) * jnp.where(odd == 1, below, above)
    columns = [column(tap, t) for t in range(4)]
    for level in range(4):
        rows[level, 0:8, :] = jnp.zeros((8, 96), F32)
        rows[level, 80:88, :] = jnp.zeros((8, 96), F32)
        total = columns[0] * rows[level, pl.ds(7, 36, stride=2), :]
        for t in range(1, 4):
            total = total + columns[t] * rows[level, pl.ds(7 + t, 36, stride=2), :]
        part = jnp.dot(total, local, precision=HIGHEST, preferred_element_type=F32)
        for e in range(2):
            at, row = (level + 4 * e) * SENT + STATS, 18 * e
            block[at : at + 8, :] = part[row : row + 8] + pltpu.roll(part[row + 8 : row + 16], 64, 1)
            block[at + 8 : at + 9, :] = part[row + 16 : row + 17] + pltpu.roll(part[row + 17 : row + 18], 64, 1)
            block[at + 9 : at + 16, :] = jnp.zeros((7, 128), F32)
    step = 16
    for which in range(2):
        copies[2 + which].wait()
        count = members.shape[1]
        for at in range(0, 432, step):
            values = [members[which, i, at : at + step, :].astype(F32) for i in range(count)]
            total = values[0]
            for value in values[1:]:
                total = total + value
            mean = total / count
            square = jnp.zeros_like(total)
            for value in values:
                dev = value - mean
                square = square + dev * dev
            full[which, at : at + step, :] = total
            full[2 + which, at : at + step, :] = square
    for k in range(8):
        for j in range(4):
            at = k * SENT + j * ROWS
            block[at : at + ROWS, :] = full[j, pl.ds(4 * ROWS * (k >> 2) + (k & 3), ROWS, stride=4), :]
    for out, distances in zip(outs, ((4,), (0, 2), (5, 1, 3), (6,), (7,))):
        for i, d in enumerate(distances):
            out[i * SENT : (i + 1) * SENT, :] = block[pl.ds(pl.multiple_of((m ^ d) * SENT, 8), SENT), :]


def merge(members, refs, out):
    sums = [ref[0:HALF, :] for ref in refs]
    total = (sums[0] + sums[1]) + (sums[2] + sums[3])
    mean = total / (4 * members)
    square = jnp.zeros_like(total)
    for one, ref in zip(sums, refs):
        dev = one / members - mean
        square = square + (ref[HALF:STATS, :] + members * (dev * dev))
    out[0:HALF, :] = total
    out[HALF:STATS, :] = square
    for s, ref in enumerate(refs):
        out[STATS + 8 * s : STATS + 8 * s + 8, :] = ref[STATS : STATS + 8, :]
        out[STATS + 32 + s : STATS + 33 + s, :] = ref[STATS + 8 : STATS + 9, :]
    out[STATS + 36 : KEPT, :] = jnp.zeros((4, 128), F32)


def merged(a, at, b, bt, count):
    one, two = a[at : at + HALF, :], b[bt : bt + HALF, :]
    diff = one - two
    squares = a[at + HALF : at + STATS, :] + b[bt + HALF : bt + STATS, :]
    return one + two, squares + diff * diff * (0.5 / count)


def merge_pair_kernel(members, ids, mine, recv, near, own, on):
    for i, out in enumerate((own, on)):
        at, bt = i * SENT, (1 + i) * SENT
        total, square = merged(mine, at, recv, bt, members)
        out[0:HALF, :] = total
        out[HALF:STATS, :] = square
        for s, (ref, to) in enumerate(((mine, at + STATS), (recv, bt + STATS))):
            out[STATS + 8 * s : STATS + 8 * s + 8, :] = ref[to : to + 8, :]
            out[STATS + 16 + s : STATS + 17 + s, :] = ref[to + 8 : to + 9, :]
        out[STATS + 18 : PAIR, :] = jnp.zeros((6, 128), F32)


def merge_on_kernel(members, ids, *refs):
    merge(members, refs[3::-1], refs[5])


def placed(share, source):
    lane = lax.broadcasted_iota(jnp.int32, share.shape, 1)
    share = jnp.where(lane < 50, share, 0.0)
    share = jnp.concatenate([share, jnp.zeros((share.shape[0], 256), F32)], axis=1)
    return pltpu.roll(share, lax.rem(48 * source + 383, 384), 1)


def placed_chunk(ref, device, count):
    wide = jnp.zeros((18, 384), F32)
    for s in range(count):
        most = ref[STATS + 8 * s : STATS + 8 * s + 8, :]
        rest = ref[STATS + 8 * count + s : STATS + 8 * count + s + 1, :]
        share = jnp.concatenate([most, pltpu.roll(most, 64, 1), rest, pltpu.roll(rest, 64, 1)], axis=0)
        wide = wide + placed(share, device ^ s)
    return wide


def put_together(one, two, count):
    diff = one[0] - two[0]
    return one[0] + two[0], one[1] + two[1] + diff * diff * (0.5 / count)


def factor_kernel(count, ids, mine, two, recv, near, late, weights, out, scratch):
    pair, more, rest = ((ref[0:HALF, :], ref[HALF:STATS, :]) for ref in (mine, two, recv))
    total, square = put_together(put_together(pair, more, count // 4), rest, count // 2)
    mean = total / count
    spread = jnp.sqrt(square / (count - 1) + 1e-06)
    prior_spread, post_spread = spread[0:ROWS], spread[ROWS:HALF]
    factor = 1.0 + 0.9 * (prior_spread - post_spread) / post_spread
    wide = placed_chunk(mine, ids[0], 2) + placed_chunk(two, ids[0] ^ 2, 2) + placed_chunk(recv, ids[0] ^ 4, 4)
    for ct in range(3):
        scratch[pl.ds(ct, 18, stride=3), :] = wide[:, 128 * ct : 128 * ct + 128]
    out[0:ROWS, :] = factor
    out[ROWS:HALF, :] = mean[0:ROWS] - factor * mean[ROWS:HALF] + scratch[...]
    shares = [
        jnp.dot(rows[...], weights[i], precision=HIGHEST, preferred_element_type=F32)
        for i, rows in enumerate((near, late))
    ]
    out[HALF:GATHER, :] = shares[0] + pltpu.roll(shares[1], 64, 1)


def join_kernel(ids, a, b, out):
    size = a.shape[0]
    out[0:size, :] = a[...]
    out[size : 2 * size, :] = b[...]


def output_kernel(ids, own, one, two, three, post, out, block, factor, base, result, sems):
    near = jnp.zeros((EDGE, 384), F32)
    late = near
    for d, ref in enumerate((own, one, two, three)):
        for i in range(2):
            at = i * GATHER
            chunk = ids[0] ^ d ^ (4 * i)
            block[pl.ds(pl.multiple_of(chunk * GATHER, 8), GATHER), :] = ref[at : at + GATHER, :]
            share = ref[at + HALF : at + GATHER, :]
            near = near + placed(share, chunk)
            late = late + placed(pltpu.roll(share, 64, 1), chunk ^ ids[2])
    for k in range(8):
        at = k * GATHER
        to = pl.ds(4 * ROWS * (k >> 2) + (k & 3), ROWS, stride=4)
        factor[to, :] = block[at : at + ROWS, :]
        base[to, :] = block[at + ROWS : at + HALF, :]
    odd = ids[1] & 1
    above = jnp.where(odd == 1, near, late)
    below = jnp.where(odd == 1, late, near)
    for ct in range(3):
        for at, part in ((4 * ct, above), (420 + 4 * ct, below)):
            base[at : at + 4, :] = base[at : at + 4, :] + part[:, 128 * ct : 128 * ct + 128]
    step, members = 48, post.shape[0]
    copies = []
    for at in range(0, 432, step):
        scale = factor[at : at + step, :]
        shift = base[at : at + step, :]
        for i in range(members):
            result[i, at : at + step, :] = (shift + scale * post[i, at : at + step, :].astype(F32)).astype(jnp.bfloat16)
        part = (slice(None), pl.ds(at, step))
        copies.append(pltpu.make_async_copy(result.at[part], out.at[part], sems.at[at // step]))
        copies[-1].start()
    for copy in copies:
        copy.wait()


def viewed(x):
    members = x.shape[0]
    x = with_layout_constraint(x.reshape(members, 4, 36, 3, 128), Layout(major_to_minor=(0, 2, 3, 1, 4)))
    return x.transpose(0, 2, 3, 1, 4).reshape(members, 432, 128)


def on_device(fine_increment, row_taps, col_weights, prior, posterior):
    mem, hor = lax.axis_size("mem"), lax.axis_size("hor")
    share = prior.shape[0]
    count = share * mem
    m, h = lax.axis_index("mem"), lax.axis_index("hor")
    middle = hor // 2
    apart = jnp.where((h == middle - 1) | (h == middle), 4, 0)
    ids = jnp.stack([m, h, apart]).astype(jnp.int32)

    def swap(x, distance):
        return lax.ppermute(x, "mem", [(i, i ^ distance) for i in range(mem)])

    def swap_rows(x, first, far=None):
        pairs = [(i, i + 1) for i in range(first, hor - 1, 2)]
        pairs = pairs + [(j, i) for i, j in pairs]
        return lax.ppermute(
            x,
            ("mem", "hor"),
            [
                (i * hor + a, (i ^ (4 if a + b == 2 * middle - 1 and far else 0)) * hor + b)
                for i in range(mem)
                for a, b in pairs
            ],
        )

    prior, posterior = viewed(prior), viewed(posterior)

    row = jax.ShapeDtypeStruct((4, 96), F32)
    packed = jnp.pad(fine_increment, ((0, 0), (0, 8), (0, 32)))
    packed = packed + jnp.pad(row_taps[:, None, :], ((0, 0), (72, 7), (0, 92)))
    on, own, *sent, near, late, weights = call(
        first_kernel,
        "first",
        ids,
        (prior, posterior, packed, col_weights),
        rows_of(SENT, 2 * SENT, 3 * SENT, SENT, SENT) + (row, row, jax.ShapeDtypeStruct((2, 96, 128), F32)),
        [
            pltpu.VMEM((2, share, 432, 128), jnp.bfloat16),
            pltpu.VMEM((4, 88, 96), F32),
            pltpu.VMEM((2, 96, 384), F32),
            pltpu.SemaphoreType.DMA((4,)),
            pltpu.VMEM((4, 432, 128), F32),
            pltpu.VMEM((8 * SENT, 128), F32),
        ],
        mib=52,
        flops=12_000_000,
        specs=[pl.BlockSpec(memory_space=pltpu.HBM)] * 2 + [VMEM, pl.BlockSpec(memory_space=pltpu.HBM)],
    )
    got = [swap(x, d) for d, x in enumerate(sent, 1)]
    near = swap_rows(near, 0)
    own, pair = call(
        functools.partial(merge_pair_kernel, share), "merge_pair", ids, (own, got[0], near), rows_of(PAIR, PAIR)
    )
    anywhere = [pl.BlockSpec(memory_space=pl.ANY)]
    send = call(
        functools.partial(merge_on_kernel, share),
        "merge_on",
        ids,
        (*got[::-1], on, pair),
        rows_of(KEPT),
        specs=[VMEM] * 4 + anywhere,
    )
    recv = swap(send, 4)
    near = call(
        functools.partial(factor_kernel, count),
        "factor",
        ids,
        (own, swap(pair, 2), recv, near, swap_rows(late, 1, True), weights),
        rows_of(GATHER),
        [pltpu.VMEM((ROWS, 128), F32)],
    )
    near = call(join_kernel, "join", ids, (near, swap(near, 4)), rows_of(2 * GATHER))
    gathered = [near] + [swap(near, distance) for distance in (1, 2, 3)]
    out = call(
        output_kernel,
        "output",
        ids,
        (*gathered, posterior),
        jax.ShapeDtypeStruct(posterior.shape, jnp.bfloat16),
        [pltpu.VMEM((8 * GATHER, 128), F32)]
        + [pltpu.VMEM((432, 128), F32)] * 2
        + [pltpu.VMEM(posterior.shape, jnp.bfloat16), pltpu.SemaphoreType.DMA((9,))],
        mib=10,
        flops=2_000_000,
        outs=pl.BlockSpec(memory_space=pltpu.HBM),
    )
    out = out.reshape(share, 36, 3, 4, 128).transpose(0, 1, 3, 2, 4)
    return out.reshape(share, 36, 4, 384).transpose(0, 2, 1, 3)


def solution(mesh):
    return jax.shard_map(
        on_device,
        mesh=mesh,
        in_specs=(
            P(None, "hor", "mem"),
            P(None, "hor"),
            P(),
            P("mem", None, "hor", None),
            P("mem", None, "hor", None),
        ),
        out_specs=P("mem", None, "hor", None),
        check_vma=False,
    )
```

```python
import functools

import jax
import jax.numpy as jnp
from jax import lax
from jax.experimental import pallas as pl
from jax.experimental.layout import Layout, with_layout_constraint
from jax.experimental.pallas import tpu as pltpu
from jax.sharding import PartitionSpec as P

ROWS = 54
HALF = 2 * ROWS
STATS = 4 * ROWS
SENT = STATS + 16
PAIR = STATS + 24
KEPT = STATS + 40
EDGE = 4
GATHER = HALF + EDGE
F32 = jnp.float32
HIGHEST = lax.Precision.HIGHEST
VMEM = pl.BlockSpec(memory_space=pltpu.VMEM)
SMEM = pl.BlockSpec(memory_space=pltpu.SMEM)


def call(kernel, name, ids, args, out, scratch=(), mib=4, flops=200_000, specs=None, outs=None, aliases=None):
    many = isinstance(out, tuple)
    moved = sum(a.size * a.dtype.itemsize for a in args) + sum(
        o.size * o.dtype.itemsize for o in (out if many else (out,))
    )
    return pl.pallas_call(
        kernel,
        out_shape=out,
        in_specs=[SMEM] + (specs or [VMEM] * len(args)),
        out_specs=tuple(outs or (VMEM,) * len(out)) if many else (outs or VMEM),
        scratch_shapes=list(scratch),
        input_output_aliases=aliases or {},
        compiler_params=pltpu.CompilerParams(vmem_limit_bytes=mib * 2**20),
        cost_estimate=pl.CostEstimate(flops=flops, bytes_accessed=moved, transcendentals=0),
        name=name,
    )(ids, *args)


def rows_of(*counts):
    shapes = tuple(jax.ShapeDtypeStruct((count, 128), F32) for count in counts)
    return shapes if len(shapes) > 1 else shapes[0]


def local_weights(own, device):
    return pltpu.roll(own, lax.rem(385 - 48 * device, 384), 1)[:, :128]


def column(taps, t):
    size = taps.shape[1]
    diagonal = lax.broadcasted_iota(jnp.int32, (size, size), 0) == lax.broadcasted_iota(jnp.int32, (size, size), 1)
    return jnp.sum(jnp.where(diagonal, taps[t : t + 1, :], 0.0), axis=1, keepdims=True)


def first_kernel(ids, prior, post, packed, weights, *refs):
    outs, (near, late, edge), (members, rows, weight, sems, full, block) = refs[:5], refs[5:8], refs[8:]
    m = ids[0]
    copies = [
        pltpu.make_async_copy(src, dst, sems.at[i])
        for i, (src, dst) in enumerate(
            (
                (weights.at[pl.ds(pl.multiple_of(96 * m, 32), 96), :], weight.at[0]),
                (weights.at[pl.ds(pl.multiple_of(96 * (m ^ ids[2]), 32), 96), :], weight.at[1]),
                *[(ref.at[pl.ds(i, 5)], members.at[j, pl.ds(i, 5)]) for j, ref in ((0, prior), (1, post)) for i in (0, 5)],
            )
        )
    ]
    for copy in copies[2:] + copies[:2]:
        copy.start()
    for copy in copies[:2]:
        copy.wait()
    tap = jnp.concatenate([packed[t, 72:73, 0:36] for t in range(4)], axis=0)
    odd = ids[1] & 1
    for level in range(4):
        rows[level, 8:80, :] = packed[level, 0:72, 0:96]
        first, last = rows[level, 8:9, :], rows[level, 79:80, :]
        near[level : level + 1, :] = jnp.where(odd == 1, first, last)
        late[level : level + 1, :] = jnp.where(odd == 1, last, first)
    local = local_weights(weight[0], m)
    above, below = tap[0:1, 0:1], tap[3:4, 35:36]
    edge[0] = local * jnp.where(odd == 1, above, below)
    edge[1] = local_weights(weight[1], m ^ ids[2]) * jnp.where(odd == 1, below, above)
    columns = [column(tap, t) for t in range(4)]
    for level in range(4):
        rows[level, 0:8, :] = jnp.zeros((8, 96), F32)
        rows[level, 80:88, :] = jnp.zeros((8, 96), F32)
        total = columns[0] * rows[level, pl.ds(7, 36, stride=2), :]
        for t in range(1, 4):
            total = total + columns[t] * rows[level, pl.ds(7 + t, 36, stride=2), :]
        part = jnp.dot(total, local, precision=HIGHEST, preferred_element_type=F32)
        for e in range(2):
            at, row = (level + 4 * e) * SENT + STATS, 18 * e
            block[at : at + 8, :] = part[row : row + 8] + pltpu.roll(part[row + 8 : row + 16], 64, 1)
            block[at + 8 : at + 9, :] = part[row + 16 : row + 17] + pltpu.roll(part[row + 17 : row + 18], 64, 1)
            block[at + 9 : at + 16, :] = jnp.zeros((7, 128), F32)
    step = 16
    for which in range(2):
        copies[2 + 2 * which].wait()
        copies[3 + 2 * which].wait()
        count = members.shape[1]
        for at in range(0, 432, step):
            values = [members[which, i, at : at + step, :].astype(F32) for i in range(count)]
            total = values[0]
            for value in values[1:]:
                total = total + value
            mean = total / count
            square = jnp.zeros_like(total)
            for value in values:
                dev = value - mean
                square = square + dev * dev
            full[which, at : at + step, :] = total
            full[2 + which, at : at + step, :] = square
    for k in range(8):
        for j in range(4):
            at = k * SENT + j * ROWS
            block[at : at + ROWS, :] = full[j, pl.ds(4 * ROWS * (k >> 2) + (k & 3), ROWS, stride=4), :]
    for out, distances in zip(outs, ((4,), (0, 2), (5, 1, 3), (6,), (7,))):
        for i, d in enumerate(distances):
            out[i * SENT : (i + 1) * SENT, :] = block[pl.ds(pl.multiple_of((m ^ d) * SENT, 8), SENT), :]


def merge(members, refs, out):
    sums = [ref[0:HALF, :] for ref in refs]
    total = (sums[0] + sums[1]) + (sums[2] + sums[3])
    mean = total / (4 * members)
    square = jnp.zeros_like(total)
    for one, ref in zip(sums, refs):
        dev = one / members - mean
        square = square + (ref[HALF:STATS, :] + members * (dev * dev))
    out[0:HALF, :] = total
    out[HALF:STATS, :] = square
    for s, ref in enumerate(refs):
        out[STATS + 8 * s : STATS + 8 * s + 8, :] = ref[STATS : STATS + 8, :]
        out[STATS + 32 + s : STATS + 33 + s, :] = ref[STATS + 8 : STATS + 9, :]
    out[STATS + 36 : KEPT, :] = jnp.zeros((4, 128), F32)


def merged(a, at, b, bt, count):
    one, two = a[at : at + HALF, :], b[bt : bt + HALF, :]
    diff = one - two
    squares = a[at + HALF : at + STATS, :] + b[bt + HALF : bt + STATS, :]
    return one + two, squares + diff * diff * (0.5 / count)


def merge_pair_kernel(members, ids, mine, recv, near, own, on):
    for i, out in enumerate((own, on)):
        at, bt = i * SENT, (1 + i) * SENT
        total, square = merged(mine, at, recv, bt, members)
        out[0:HALF, :] = total
        out[HALF:STATS, :] = square
        for s, (ref, to) in enumerate(((mine, at + STATS), (recv, bt + STATS))):
            out[STATS + 8 * s : STATS + 8 * s + 8, :] = ref[to : to + 8, :]
            out[STATS + 16 + s : STATS + 17 + s, :] = ref[to + 8 : to + 9, :]
        out[STATS + 18 : PAIR, :] = jnp.zeros((6, 128), F32)


def merge_on_kernel(members, ids, *refs):
    merge(members, refs[3::-1], refs[5])


def placed(share, source):
    lane = lax.broadcasted_iota(jnp.int32, share.shape, 1)
    share = jnp.where(lane < 50, share, 0.0)
    share = jnp.concatenate([share, jnp.zeros((share.shape[0], 256), F32)], axis=1)
    return pltpu.roll(share, lax.rem(48 * source + 383, 384), 1)


def placed_chunk(ref, device, count):
    wide = jnp.zeros((18, 384), F32)
    for s in range(count):
        most = ref[STATS + 8 * s : STATS + 8 * s + 8, :]
        rest = ref[STATS + 8 * count + s : STATS + 8 * count + s + 1, :]
        share = jnp.concatenate([most, pltpu.roll(most, 64, 1), rest, pltpu.roll(rest, 64, 1)], axis=0)
        wide = wide + placed(share, device ^ s)
    return wide


def put_together(one, two, count):
    diff = one[0] - two[0]
    return one[0] + two[0], one[1] + two[1] + diff * diff * (0.5 / count)


def factor_kernel(count, ids, mine, two, recv, near, late, weights, out, scratch):
    pair, more, rest = ((ref[0:HALF, :], ref[HALF:STATS, :]) for ref in (mine, two, recv))
    total, square = put_together(put_together(pair, more, count // 4), rest, count // 2)
    mean = total / count
    spread = jnp.sqrt(square / (count - 1) + 1e-06)
    prior_spread, post_spread = spread[0:ROWS], spread[ROWS:HALF]
    factor = 1.0 + 0.9 * (prior_spread - post_spread) / post_spread
    wide = placed_chunk(mine, ids[0], 2) + placed_chunk(two, ids[0] ^ 2, 2) + placed_chunk(recv, ids[0] ^ 4, 4)
    for ct in range(3):
        scratch[pl.ds(ct, 18, stride=3), :] = wide[:, 128 * ct : 128 * ct + 128]
    out[0:ROWS, :] = factor
    out[ROWS:HALF, :] = mean[0:ROWS] - factor * mean[ROWS:HALF] + scratch[...]
    shares = [
        jnp.dot(rows[...], weights[i], precision=HIGHEST, preferred_element_type=F32)
        for i, rows in enumerate((near, late))
    ]
    out[HALF:GATHER, :] = shares[0] + pltpu.roll(shares[1], 64, 1)


def join_kernel(ids, a, b, out):
    size = a.shape[0]
    out[0:size, :] = a[...]
    out[size : 2 * size, :] = b[...]


def output_kernel(ids, own, one, two, three, post, out, block, factor, base, result, sems):
    near = jnp.zeros((EDGE, 384), F32)
    late = near
    for d, ref in enumerate((own, one, two, three)):
        for i in range(2):
            at = i * GATHER
            chunk = ids[0] ^ d ^ (4 * i)
            block[pl.ds(pl.multiple_of(chunk * GATHER, 8), GATHER), :] = ref[at : at + GATHER, :]
            share = ref[at + HALF : at + GATHER, :]
            near = near + placed(share, chunk)
            late = late + placed(pltpu.roll(share, 64, 1), chunk ^ ids[2])
    for k in range(8):
        at = k * GATHER
        to = pl.ds(4 * ROWS * (k >> 2) + (k & 3), ROWS, stride=4)
        factor[to, :] = block[at : at + ROWS, :]
        base[to, :] = block[at + ROWS : at + HALF, :]
    odd = ids[1] & 1
    above = jnp.where(odd == 1, near, late)
    below = jnp.where(odd == 1, late, near)
    for ct in range(3):
        for at, part in ((4 * ct, above), (420 + 4 * ct, below)):
            base[at : at + 4, :] = base[at : at + 4, :] + part[:, 128 * ct : 128 * ct + 128]
    step, members = 48, post.shape[0]
    copies = []
    for at in range(0, 432, step):
        scale = factor[at : at + step, :]
        shift = base[at : at + step, :]
        for i in range(members):
            result[i, at : at + step, :] = (shift + scale * post[i, at : at + step, :].astype(F32)).astype(jnp.bfloat16)
        part = (slice(None), pl.ds(at, step))
        copies.append(pltpu.make_async_copy(result.at[part], out.at[part], sems.at[at // step]))
        copies[-1].start()
    for copy in copies:
        copy.wait()


def viewed(x):
    members = x.shape[0]
    x = with_layout_constraint(x.reshape(members, 4, 36, 3, 128), Layout(major_to_minor=(0, 2, 3, 1, 4)))
    return x.transpose(0, 2, 3, 1, 4).reshape(members, 432, 128)


def on_device(fine_increment, row_taps, col_weights, prior, posterior):
    mem, hor = lax.axis_size("mem"), lax.axis_size("hor")
    share = prior.shape[0]
    count = share * mem
    m, h = lax.axis_index("mem"), lax.axis_index("hor")
    middle = hor // 2
    apart = jnp.where((h == middle - 1) | (h == middle), 4, 0)
    ids = jnp.stack([m, h, apart]).astype(jnp.int32)

    def swap(x, distance):
        return lax.ppermute(x, "mem", [(i, i ^ distance) for i in range(mem)])

    def swap_rows(x, first, far=None):
        pairs = [(i, i + 1) for i in range(first, hor - 1, 2)]
        pairs = pairs + [(j, i) for i, j in pairs]
        return lax.ppermute(
            x,
            ("mem", "hor"),
            [
                (i * hor + a, (i ^ (4 if a + b == 2 * middle - 1 and far else 0)) * hor + b)
                for i in range(mem)
                for a, b in pairs
            ],
        )

    prior, posterior = viewed(prior), viewed(posterior)

    row = jax.ShapeDtypeStruct((4, 96), F32)
    packed = jnp.pad(fine_increment, ((0, 0), (0, 8), (0, 32)))
    packed = packed + jnp.pad(row_taps[:, None, :], ((0, 0), (72, 7), (0, 92)))
    on, own, *sent, near, late, weights = call(
        first_kernel,
        "first",
        ids,
        (prior, posterior, packed, col_weights),
        rows_of(SENT, 2 * SENT, 3 * SENT, SENT, SENT) + (row, row, jax.ShapeDtypeStruct((2, 96, 128), F32)),
        [
            pltpu.VMEM((2, share, 432, 128), jnp.bfloat16),
            pltpu.VMEM((4, 88, 96), F32),
            pltpu.VMEM((2, 96, 384), F32),
            pltpu.SemaphoreType.DMA((6,)),
            pltpu.VMEM((4, 432, 128), F32),
            pltpu.VMEM((8 * SENT, 128), F32),
        ],
        mib=52,
        flops=12_000_000,
        specs=[pl.BlockSpec(memory_space=pltpu.HBM)] * 2 + [VMEM, pl.BlockSpec(memory_space=pltpu.HBM)],
    )
    got = [swap(x, d) for d, x in enumerate(sent, 1)]
    near = swap_rows(near, 0)
    own, pair = call(
        functools.partial(merge_pair_kernel, share), "merge_pair", ids, (own, got[0], near), rows_of(PAIR, PAIR)
    )
    anywhere = [pl.BlockSpec(memory_space=pl.ANY)]
    send = call(
        functools.partial(merge_on_kernel, share),
        "merge_on",
        ids,
        (*got[::-1], on, pair),
        rows_of(KEPT),
        specs=[VMEM] * 4 + anywhere,
    )
    recv = swap(send, 4)
    near = call(
        functools.partial(factor_kernel, count),
        "factor",
        ids,
        (own, swap(pair, 2), recv, near, swap_rows(late, 1, True), weights),
        rows_of(GATHER),
        [pltpu.VMEM((ROWS, 128), F32)],
    )
    near = call(join_kernel, "join", ids, (near, swap(near, 4)), rows_of(2 * GATHER))
    gathered = [near] + [swap(near, distance) for distance in (1, 2, 3)]
    out = call(
        output_kernel,
        "output",
        ids,
        (*gathered, posterior),
        jax.ShapeDtypeStruct(posterior.shape, jnp.bfloat16),
        [pltpu.VMEM((8 * GATHER, 128), F32)]
        + [pltpu.VMEM((432, 128), F32)] * 2
        + [pltpu.VMEM(posterior.shape, jnp.bfloat16), pltpu.SemaphoreType.DMA((9,))],
        mib=10,
        flops=2_000_000,
        outs=pl.BlockSpec(memory_space=pltpu.HBM),
    )
    out = out.reshape(share, 36, 3, 4, 128).transpose(0, 1, 3, 2, 4)
    return out.reshape(share, 36, 4, 384).transpose(0, 2, 1, 3)


def solution(mesh):
    return jax.shard_map(
        on_device,
        mesh=mesh,
        in_specs=(
            P(None, "hor", "mem"),
            P(None, "hor"),
            P(),
            P("mem", None, "hor", None),
            P("mem", None, "hor", None),
        ),
        out_specs=P("mem", None, "hor", None),
        check_vma=False,
    )
```
